512 devices in a mesh: tm: 32 (over x, y), region: 16 (over z, core).
Axes of the slice: x: 4, y: 8, z: 8, core: 2. Of those that a mesh axis runs over, the one named last changes fastest.
Arguments:
- events: float32 [32, 16, 4, 3072], P('tm', 'region'), may hold values from 0 to 32, as said below
- background: float32 [32, 16, 3072], P('tm', 'region'), may hold values from 0.1 to 2
- decays: float32 [16], replicated, may hold values from 0.3 to 30
- widths: float32 [16], replicated, may hold values from 0.05 to 1.5
- mix_start: float32 [16, 16], replicated, may hold values from 0.0005 to 0.006
- rate_start: float32 [1], replicated, may hold values from 0.3 to 3
- pair_block: int32 [32, 16, 6], P('tm', 'region'), may hold values from 0 to 23, as said below
- pair_source: int32 [32, 16, 6], P('tm', 'region'), may hold values from 0 to 287, as said below
- pair_count: int32 [32, 16], P('tm', 'region'), may hold values from 1 to 6, as said below
Outputs:
- mixture: float32 [16, 16], replicated
- base_rate: float32 [1], replicated
- bg_share: float32 [32, 16, 3072], P('tm', 'region')
- offspring: float32 [32, 16, 3072], P('tm', 'region')
The draws below stay inside these ranges and needn't reach their ends.
Inputs may be any that keep to these rules, and one draw needn't show every extreme that they name: `events`: rows per event: time, in [s, s + 1) on slab s; east position, in [r, r + 1) on region r; north position in [0, 1); magnitude above the threshold in [0, 2]. `pair_block`: a block of the device that holds the slot. `pair_source`: (d * 3 + e) * 24 + b with d < 4; it always names a slab s - d >= 0 and a region r + e - 1 that exist, also in slots that are not live. `pair_count`: some device uses all 6 slots in every draw.
All inputs are finite; a program needn't handle non-finite values.
Results may differ from the reference program's by a relative error of at most 0.0003.
Values sent between devices are 32-bit elements; how exact they have to be, the bound alone decides.
A program may use at most 64 MiB of HBM per device.

```python
import math
import jax
import jax.numpy as jnp
from jax import lax

NDECAY = 16
NWIDTH = 16
BLK = 128
NBLK = 24
EDEV = 3072
DEPTH = 4
PMAX = 6
ITERS = 2
EVENTS = 1572864
N_TM = 32
N_REGION = 16


def draw_events(key, part):
    key = jax.random.fold_in(key, 11)
    subkeys = jax.random.split(key, 4)
    grid_shape = (N_TM, N_REGION, NBLK * BLK)
    slab_index = jnp.arange(N_TM, dtype=jnp.float32)[:, None, None]
    zone_index = jnp.arange(N_REGION, dtype=jnp.float32)[None, :, None]
    draw_a = jax.random.uniform(subkeys[0], grid_shape, jnp.float32, 0.0, 0.999)
    draw_b = jax.random.uniform(subkeys[1], grid_shape, jnp.float32, 0.0, 0.999)
    draw_c = jax.random.uniform(subkeys[2], grid_shape, jnp.float32, 0.0, 0.999)
    draw_d = jax.random.uniform(subkeys[3], grid_shape, jnp.float32, 0.0, 1.0)
    event_time = slab_index + draw_a
    north_pos = draw_c
    magnitude = -0.8 * jnp.log(1.0 - 0.9 * draw_d)
    east_pos = zone_index + draw_b
    return jnp.stack([event_time, east_pos, north_pos, magnitude], axis=2)


def draw_pair_block(key, part):
    key = jax.random.fold_in(key, 12)
    return jax.random.randint(key, (N_TM, N_REGION, PMAX), 0, NBLK, dtype=jnp.int32)


def draw_pair_source(key, part):
    key = jax.random.fold_in(key, 13)
    subkeys = jax.random.split(key, 3)
    grid_shape = (N_TM, N_REGION, PMAX)
    slab_index = jnp.broadcast_to(jnp.arange(N_TM, dtype=jnp.int32)[:, None, None], grid_shape)
    zone_index = jnp.broadcast_to(jnp.arange(N_REGION, dtype=jnp.int32)[None, :, None], grid_shape)
    time_lag = jax.random.randint(subkeys[0], grid_shape, 0, jnp.minimum(DEPTH, slab_index + 1), dtype=jnp.int32)
    lower_side = jnp.where(zone_index > 0, 0, 1).astype(jnp.int32)
    upper_side = jnp.where(zone_index < N_REGION - 1, 3, 2).astype(jnp.int32)
    region_side = jax.random.randint(subkeys[1], grid_shape, lower_side, upper_side, dtype=jnp.int32)
    source_blk = jax.random.randint(subkeys[2], grid_shape, 0, NBLK, dtype=jnp.int32)
    return (time_lag * 3 + region_side) * NBLK + source_blk


def draw_pair_count(key, part):
    key = jax.random.fold_in(key, 14)
    subkeys = jax.random.split(key, 3)
    grid_shape = (N_TM, N_REGION)
    quiet_load = jax.random.randint(subkeys[0], grid_shape, 1, max(PMAX // 2, 1) + 1, dtype=jnp.int32)
    bursty = jax.random.randint(subkeys[1], grid_shape, 0, 4, dtype=jnp.int32) == 0
    counts = jnp.where(bursty, PMAX, quiet_load).astype(jnp.int32)
    full_device = jax.random.randint(subkeys[2], (), 0, N_TM * N_REGION, dtype=jnp.int32)
    return counts.reshape(-1).at[full_device].set(PMAX).reshape(grid_shape)


def steps_of(stream_key, shape, shards, smallest, largest):
    gain = 1.0
    for dim, shards_of in shards:
        draws = jax.random.uniform(jax.random.fold_in(jax.random.fold_in(stream_key, 6), dim), (shards_of,), jnp.float32, smallest / len(shards), largest / len(shards))
        gain = gain * jnp.repeat(jnp.exp(draws), shape[dim] // shards_of).reshape((-1,) + (1,) * (len(shape) - 1 - dim))
    return gain


def setup_inputs(seed: int = 0) -> dict:
    splits = jax.random.split(jax.random.key(seed), 10)
    events = draw_events(jax.random.fold_in(splits[9], 71), 0)
    background = jnp.clip(jnp.exp(math.log(2.0) - 2.9957323 * jax.random.uniform(splits[1], (N_TM, N_REGION, EDEV), jnp.float32) ** steps_of(splits[1], (N_TM, N_REGION, EDEV), ((0, 32), (1, 16)), -0.2, 0.2)), 0.1, 2.0)
    decays = jnp.clip(jnp.exp(jax.random.uniform(splits[2], (NDECAY,), jnp.float32, math.log(0.3), math.log(30.0))), 0.3, 30.0)
    widths = jnp.clip(jnp.exp(jax.random.uniform(splits[3], (NWIDTH,), jnp.float32, math.log(0.05), math.log(1.5))), 0.05, 1.5)
    mix_start = jnp.clip(jnp.exp(jax.random.uniform(splits[4], (NDECAY, NWIDTH), jnp.float32, math.log(0.0005), math.log(0.006))), 0.0005, 0.006)
    rate_start = jnp.clip(jnp.exp(jax.random.uniform(splits[5], (1,), jnp.float32, math.log(0.3), math.log(3.0))), 0.3, 3.0)
    pair_block = draw_pair_block(jax.random.fold_in(splits[9], 71), 0)
    pair_source = draw_pair_source(jax.random.fold_in(splits[9], 71), 0)
    pair_count = draw_pair_count(jax.random.fold_in(splits[9], 71), 0)
    return {"events": events, "background": background, "decays": decays, "widths": widths, "mix_start": mix_start, "rate_start": rate_start, "pair_block": pair_block, "pair_source": pair_source, "pair_count": pair_count}


PRODUCTIVITY = 1.0


def pair_tiles(target, source, decays, widths):
    gap_time = target[0][:, None] - source[0][None, :]
    gap_east = target[1][:, None] - source[1][None, :]
    gap_north = target[2][:, None] - source[2][None, :]
    causal = gap_time > 0.0
    elapsed = jnp.where(causal, gap_time, 0.0)
    temporal = jnp.where(causal[None], decays[:, None, None] * jnp.exp(-decays[:, None, None] * elapsed[None]), 0.0)
    spread = 2.0 * widths * widths
    spatial = jnp.exp(-(gap_east * gap_east + gap_north * gap_north)[None] / spread[:, None, None]) / (math.pi * spread)[:, None, None]
    return temporal, spatial


def excitation(temporal, spatial, mixture, yields):
    weighted = jnp.einsum("kl,lij->kij", mixture, spatial, precision=lax.Precision.HIGHEST)
    return jnp.sum(temporal * weighted, axis=0) * yields[None, :]


def mass_split(temporal, spatial, weights):
    return jnp.einsum("kij,lij->kl", temporal * weights[None], spatial, precision=lax.Precision.HIGHEST)


def reference(events, background, decays, widths, mix_start, rate_start, pair_block, pair_source, pair_count):
    block_count = EDEV // BLK
    blocks = events.reshape(N_TM, N_REGION, 4, block_count, BLK)
    grid_shape = pair_block.shape
    tgt_slab = jnp.broadcast_to(jnp.arange(N_TM, dtype=jnp.int32)[:, None, None], grid_shape).reshape(-1)
    tgt_zone = jnp.broadcast_to(jnp.arange(N_REGION, dtype=jnp.int32)[None, :, None], grid_shape).reshape(-1)
    slot_index = jnp.broadcast_to(jnp.arange(PMAX, dtype=jnp.int32)[None, None, :], grid_shape)
    live_flag = (slot_index < pair_count[:, :, None]).astype(jnp.float32).reshape(-1)
    tgt_block = pair_block.reshape(-1).astype(jnp.int32)
    candidate = pair_source.reshape(-1).astype(jnp.int32)
    time_lag = candidate // (3 * block_count)
    region_side = (candidate // block_count) % 3
    src_block = candidate % block_count
    src_slab = jnp.clip(tgt_slab - time_lag, 0, N_TM - 1)
    src_zone = jnp.clip(tgt_zone + region_side - 1, 0, N_REGION - 1)
    listing = (tgt_slab, tgt_zone, tgt_block, src_slab, src_zone, src_block, live_flag)
    yield_total = jnp.sum(jnp.exp(PRODUCTIVITY * events[:, :, 3, :]))
    base_level = background.reshape(N_TM, N_REGION, block_count, BLK)

    def tiles_of(pair_item):
        target = blocks[pair_item[0], pair_item[1]][:, pair_item[2]]
        source = blocks[pair_item[3], pair_item[4]][:, pair_item[5]]
        temporal, spatial = pair_tiles(target, source, decays, widths)
        return temporal, spatial, jnp.exp(PRODUCTIVITY * source[3])

    mixture = mix_start
    base_rate = rate_start[0]
    bg_share = base_level
    offspring = base_level
    for sweep in range(ITERS):
        def add_trigger(running, pair_item):
            temporal, spatial, yields = tiles_of(pair_item)
            row_sums = jnp.sum(excitation(temporal, spatial, mixture, yields), axis=1) * pair_item[6]
            return running.at[pair_item[0], pair_item[1], pair_item[2]].add(row_sums), None

        triggered, _ = lax.scan(add_trigger, jnp.zeros((N_TM, N_REGION, block_count, BLK), jnp.float32), listing)
        intensity = base_rate * base_level + triggered
        inverse = 1.0 / intensity

        def split_pair(carry, pair_item):
            scores, spent = carry
            temporal, spatial, yields = tiles_of(pair_item)
            weights = inverse[pair_item[0], pair_item[1], pair_item[2]] * pair_item[6]
            trigger = excitation(temporal, spatial, mixture, yields) * weights[:, None]
            spent = spent.at[pair_item[3], pair_item[4], pair_item[5]].add(jnp.sum(trigger, axis=0))
            scores = scores + mass_split(temporal, spatial, weights[:, None] * yields[None, :])
            return (scores, spent), None

        initial = (jnp.zeros((NDECAY, NWIDTH), jnp.float32), jnp.zeros((N_TM, N_REGION, block_count, BLK), jnp.float32))
        (scores, offspring), _ = lax.scan(split_pair, initial, listing)
        bg_share = base_rate * base_level * inverse
        mixture = mixture * scores / yield_total
        base_rate = jnp.sum(bg_share) / EVENTS
    return (mixture, jnp.reshape(base_rate, (1,)), bg_share.reshape(N_TM, N_REGION, EDEV), offspring.reshape(N_TM, N_REGION, EDEV))
```

```python
import math

import jax
import jax.numpy as jnp
from jax import lax
from jax.experimental import pallas as pl
from jax.experimental.pallas import tpu as pltpu
from jax.sharding import PartitionSpec as P

NK = 16
NL = 16
BLK = 128
NBLK = 24
DEPTH = 4
PMAX = 6
ITERS = 2
CELL = 3 * NBLK
NEAR = 3 * DEPTH - 1
FAR = 1.0e6
MESH = pl.DeviceIdType.MESH
PRODUCTIVITY = 1.0


def split_bf16(value):
    high = value.astype(jnp.bfloat16)
    low = (value - high.astype(jnp.float32)).astype(jnp.bfloat16)
    return high, low


def stacked_rows(value):
    high, low = split_bf16(value)
    return jnp.concatenate(
        [
            jnp.concatenate([high, high], axis=1),
            jnp.concatenate([low, jnp.zeros_like(low)], axis=1),
        ],
        axis=0,
    )


def columns(rows):
    return jnp.transpose(jnp.concatenate([rows, rows], axis=0))


def kernel(
    n_tm,
    n_region,
    ev_in,
    bg_in,
    decays_in,
    widths_in,
    mix_in,
    rate_s,
    block_in,
    source_in,
    count_s,
    mix_out,
    rate_out,
    share_out,
    offspring_out,
    bg_ref,
    decays_s,
    widths_s,
    mix_ref,
    block_s,
    source_s,
    events,
    request,
    requests,
    requests_s,
    answer,
    picked,
    falloff,
    stats,
    early,
    late,
    coeff,
    payload,
    partial,
    returned,
    local_sem,
    request_send,
    request_recv,
    event_send,
    event_recv,
    answer_send,
    answer_recv,
    return_send,
    return_recv,
    sum_send,
    sum_recv,
):
    slab = lax.axis_index("tm")
    zone = lax.axis_index("region")
    events_all = float(n_tm * n_region * NBLK * BLK)
    lengths = (n_region, n_tm)
    my_place = (zone, slab)

    def wrapped(place, step, length):
        moved = place + step
        return jnp.where(moved >= length, moved - length, jnp.where(moved < 0, moved + length, moved))

    def device(lag, side):
        return (wrapped(slab, lag, n_tm), wrapped(zone, side, n_region))

    def peer(axis, step):
        if axis == 0:
            return (slab, wrapped(zone, step, n_region))
        return (wrapped(slab, step, n_tm), zone)

    staged = (
        (source_in, source_s),
        (block_in, block_s),
        (decays_in, decays_s),
        (widths_in, widths_s),
        (mix_in, mix_ref),
        (bg_in, bg_ref),
        (ev_in, events.at[pl.ds(NBLK, NBLK)]),
    )
    staging = [
        pltpu.make_async_copy(src, dst, local_sem.at[index])
        for index, (src, dst) in enumerate(staged)
    ]
    for copy in staging:
        copy.start()

    barrier = pltpu.get_barrier_semaphore()
    near = [(lag, 0) for lag in range(1, DEPTH)]
    near += [(lag, side) for lag in range(DEPTH) for side in (-1, 1)]
    greeted = [(-lag, side) for lag, side in near] + [(lag, -side) for lag, side in near if lag]
    greeted += [(0, step) for step in range(2, n_region - 1)]
    greeted += [(step, 0) for step in range(DEPTH, n_tm - DEPTH + 1)]
    for place in greeted:
        pl.semaphore_signal(barrier, inc=1, device_id=device(*place), device_id_type=MESH)
    staging[0].wait()
    lane = lax.broadcasted_iota(jnp.int32, (1, BLK), 1)
    asked = jnp.zeros((1, BLK), jnp.int32)
    for p in range(PMAX):
        asked = jnp.where(lane == p, source_s[0, 0, p], asked)
    request[...] = asked
    pl.semaphore_wait(barrier, len(greeted))

    pending = []

    def send(src, dst, send_sem, recv_sem, device):
        copy = pltpu.make_async_remote_copy(
            src_ref=src,
            dst_ref=dst,
            send_sem=send_sem,
            recv_sem=recv_sem,
            device_id=device,
            device_id_type=MESH,
        )
        copy.start()
        pending.append(copy)
        return copy

    event_copies = [
        send(
            ev_in,
            events.at[pl.ds(2 * NBLK * side, NBLK)],
            event_send.at[side],
            event_recv.at[side],
            device(0, 1 - 2 * side),
        )
        for side in range(2)
    ]
    request_copies = [
        send(
            request,
            requests.at[index],
            request_send.at[index],
            request_recv.at[index],
            device(-lag, side),
        )
        for index, (lag, side) in enumerate(near)
    ]

    for copy in staging[1:]:
        copy.wait()
    decay_col = jnp.zeros((NK, BLK), jnp.float32)
    row16 = lax.broadcasted_iota(jnp.int32, (NK, BLK), 0)
    for k in range(NK):
        decay_col = jnp.where(row16 == k, decays_s[k], decay_col)
    width_col = jnp.zeros((NL, BLK), jnp.float32)
    for l in range(NL):
        width_col = jnp.where(row16 == l, widths_s[l], width_col)
    spread = 2.0 * width_col * width_col
    coeff[0] = -math.log2(math.e) / spread
    coeff[1] = 1.0 / (math.pi * spread)
    mix_tile = mix_ref[...]
    mixture = [jnp.broadcast_to(mix_tile[:, l : l + 1], (NK, BLK)) for l in range(NL)]
    mixture = jnp.concatenate(mixture, axis=0)
    own_yield = jnp.sum(jnp.exp(PRODUCTIVITY * events[pl.ds(NBLK, NBLK), 3, :]), axis=0, keepdims=True)
    own_yield = jnp.broadcast_to(jnp.sum(own_yield, axis=1, keepdims=True), (1, BLK))

    askers = DEPTH - 1
    for copy in request_copies[:askers]:
        copy.wait_recv()
    scalar_copies = [
        pltpu.make_async_copy(requests.at[part], requests_s.at[part], local_sem.at[len(staged) + half])
        for half, part in enumerate((pl.ds(0, askers), pl.ds(askers, len(near) - askers)))
    ]
    scalar_copies[0].start()
    scalar_copies[0].wait()
    for copy in event_copies:
        copy.wait_recv()

    def cell_of(relative):
        inside = jnp.logical_and(relative >= 0, relative < CELL)
        return jnp.where(inside, relative, 0)

    answer_copies = []
    for lag in range(DEPTH - 1, 0, -1):
        for p in range(PMAX):
            answer[lag - 1, p] = events[cell_of(requests_s[lag - 1, 0, p] - lag * CELL)]
        answer_copies.append(
            send(
                answer.at[lag - 1],
                picked.at[lag],
                answer_send.at[lag - 1],
                answer_recv.at[lag - 1],
                device(lag, 0),
            )
        )
    for p in range(PMAX):
        picked[0, p] = events[cell_of(source_s[0, 0, p])]
    for copy in answer_copies:
        copy.wait_recv()

    start_time = slab.astype(jnp.float32)
    live_count = count_s[0, 0]

    def members(p):
        candidate = source_s[0, 0, p]
        lag = (
            (candidate >= CELL).astype(jnp.int32)
            + (candidate >= 2 * CELL).astype(jnp.int32)
            + (candidate >= 3 * CELL).astype(jnp.int32)
        )
        return picked[lag, p], events[NBLK + block_s[0, 0, p]]

    def distances(target, source):
        gap_time = target[0] - source[0]
        gap_east = target[1] - source[1]
        gap_north = target[2] - source[2]
        square = gap_east * gap_east + gap_north * gap_north
        return jnp.where(gap_time > 0.0, square, FAR)

    def fall(square, l):
        return split_bf16(jnp.exp2(square * coeff[0, l : l + 1, :]))

    def prepare(p, carry):
        source, target = members(p)
        live = jnp.where(p < live_count, 1.0, 0.0)
        after = decay_col * jnp.exp(-decay_col * (target[0:1] - start_time)) * live
        before = jnp.exp(decay_col * (source[0:1] - start_time)) * jnp.exp(PRODUCTIVITY * source[3:4])
        late[p] = after
        early[p] = before
        left = stacked_rows(before)
        cols = columns(source)
        square = distances(
            [target[c : c + 1] for c in range(3)], [cols[:, c : c + 1] for c in range(3)]
        )
        for pair in range(NL // 2):
            parts = [
                jnp.concatenate(fall(square, l), axis=0) for l in (2 * pair, 2 * pair + 1)
            ]
            right = jnp.concatenate(parts, axis=1)
            both = jnp.dot(left, right, preferred_element_type=jnp.float32)
            both = both[:NK] + both[NK:]
            for side in range(2):
                l = 2 * pair + side
                stats[p, l * NK : (l + 1) * NK, :] = (
                    both[:, side * BLK : (side + 1) * BLK] * after * coeff[1, l : l + 1, :]
                )
        return carry

    lax.fori_loop(0, PMAX, prepare, 0)

    def prepare_back(p, carry):
        source, target = members(p)
        cols = columns(target)
        square = distances(
            [cols[:, c : c + 1] for c in range(3)], [source[c : c + 1] for c in range(3)]
        )
        for l in range(NL):
            falloff[p, l, 0], falloff[p, l, 1] = fall(square, l)
        return carry

    block_row = lax.broadcasted_iota(jnp.int32, (NBLK, BLK), 0)
    background = bg_ref[...]

    def expect(mixture, rate):
        triggered = jnp.zeros((NBLK, BLK), jnp.float32)
        for p in range(PMAX):
            row = jnp.sum(stats[p] * mixture, axis=0, keepdims=True)
            triggered = triggered + jnp.where(block_row == block_s[0, 0, p], row, 0.0)
        level = rate * background
        inverse = 1.0 / (level + triggered)
        share = level * inverse
        weights = [
            jnp.sum(jnp.where(block_row == block_s[0, 0, p], inverse, 0.0), axis=0, keepdims=True)
            for p in range(PMAX)
        ]
        scores = stats[0] * weights[0]
        for p in range(1, PMAX):
            scores = scores + stats[p] * weights[p]
        rows = [
            jnp.sum(jnp.transpose(scores[half * BLK : (half + 1) * BLK]), axis=0, keepdims=True)
            for half in range(2)
        ]
        total = jnp.sum(jnp.sum(share, axis=0, keepdims=True), axis=1, keepdims=True)
        rows.append(jnp.broadcast_to(total, (1, BLK)))
        rows.append(own_yield)
        return share, weights, jnp.concatenate(rows, axis=0)

    def start_sum(stage, axis, value):
        payload[stage] = value
        partial[stage, my_place[axis]] = value
        for step in range(1, lengths[axis]):
            pltpu.make_async_remote_copy(
                src_ref=payload.at[stage],
                dst_ref=partial.at[stage, my_place[axis]],
                send_sem=sum_send.at[stage],
                recv_sem=sum_recv.at[stage],
                device_id=peer(axis, step),
                device_id_type=MESH,
            ).start()

    def others(stage, axis, sems):
        part = partial.at[stage, pl.ds(0, lengths[axis] - 1)]
        return pltpu.make_async_copy(part, part, sems.at[stage])

    def end_sum(stage, axis):
        others(stage, axis, sum_recv).wait()
        return jnp.sum(partial[stage, 0 : lengths[axis]], axis=0)

    def update(mixture, total):
        cols = columns(total)
        factor = jnp.concatenate(
            [jnp.broadcast_to(cols[:, half : half + 1], (BLK, BLK)) for half in range(2)], axis=0
        )
        return mixture * factor / total[3:4, :], total[2:3, :] / events_all

    share, weights, value = expect(mixture, jnp.full((1, BLK), rate_s[0], jnp.float32))
    for axis in range(2):
        start_sum(axis, axis, value)
        lax.fori_loop(axis * PMAX // 2, (axis + 1) * PMAX // 2, prepare_back, 0)
        if axis == 0:
            for copy in request_copies[askers:]:
                copy.wait_recv()
            scalar_copies[1].start()
        else:
            scalar_copies[1].wait()
            for copy in pending:
                copy.wait_send()
            pending.clear()
        value = end_sum(axis, axis)
    mixture, rate = update(mixture, value)

    share, weights, value = expect(mixture, rate)
    start_sum(2, 0, value)
    share_out[...] = share
    scaled = mixture * jnp.concatenate(
        [jnp.broadcast_to(coeff[1, l : l + 1, :], (NK, BLK)) for l in range(NL)], axis=0
    )

    for p in range(PMAX):
        late[p] = late[p] * weights[p]

    stats[0] = scaled

    def give_back(p, rows):
        left = stacked_rows(late[p])
        gathered = jnp.zeros((NK, BLK), jnp.float32)
        for pair in range(NL // 2):
            right = jnp.concatenate(
                [
                    jnp.concatenate([falloff[p, l, 0], falloff[p, l, 1]], axis=0)
                    for l in (2 * pair, 2 * pair + 1)
                ],
                axis=1,
            )
            both = jnp.dot(left, right, preferred_element_type=jnp.float32)
            both = both[:NK] + both[NK:]
            for side in range(2):
                l = 2 * pair + side
                gathered = gathered + both[:, side * BLK : (side + 1) * BLK] * stats[0, l * NK : (l + 1) * NK, :]
        row = jnp.sum(gathered * early[p], axis=0, keepdims=True)
        return jnp.where(lax.broadcasted_iota(jnp.int32, (8, BLK), 0) == p, row, rows)

    rows = lax.fori_loop(0, PMAX, give_back, jnp.zeros((8, BLK), jnp.float32))
    returned[0] = rows
    return_copies = [
        send(
            returned.at[0],
            returned.at[index + 1],
            return_send.at[index],
            return_recv.at[index],
            device(-lag, side),
        )
        for index, (lag, side) in enumerate(near)
    ]
    value = end_sum(2, 0)
    start_sum(3, 1, value)

    for copy in return_copies:
        copy.wait_recv()
    gathered = jnp.zeros((NBLK, BLK), jnp.float32)
    for index, (lag, side) in enumerate([(0, 0)] + near):
        first = (lag * 3 + side + 1) * NBLK
        for p in range(PMAX):
            named = source_s[0, 0, p] if index == 0 else requests_s[index - 1, 0, p]
            gathered = gathered + jnp.where(
                block_row == named - first, returned[index, p : p + 1, :], 0.0
            )
    offspring_out[...] = gathered
    for copy in pending:
        copy.wait_send()
    for stage in range(3):
        others(stage, stage % 2, sum_send).wait()
    value = end_sum(3, 1)
    others(3, 1, sum_send).wait()
    mixture, rate = update(mixture, value)
    lane16 = lax.broadcasted_iota(jnp.int32, (NK, BLK), 1)
    square_mix = jnp.zeros((NK, BLK), jnp.float32)
    for l in range(NL):
        square_mix = jnp.where(lane16 == l, mixture[l * NK : (l + 1) * NK], square_mix)
    mix_out[...] = square_mix[:, :NL]
    rate_out[...] = rate[:, 0:1]


def finish(*refs):
    arrived, handed, sems = refs[:4], refs[4:8], refs[8]
    copies = [
        pltpu.make_async_copy(src, dst, sems.at[index])
        for index, (src, dst) in enumerate(zip(arrived, handed))
    ]
    for copy in copies:
        copy.start()
    for copy in copies:
        copy.wait()


def solution(mesh):
    n_tm, n_region = mesh.shape["tm"], mesh.shape["region"]

    def body(
        events, background, decays, widths, mix_start, rate_start, pair_block, pair_source, pair_count
    ):
        blocks = jnp.transpose(jnp.reshape(events, (4, NBLK, BLK)), (1, 0, 2))
        smem = pl.BlockSpec(memory_space=pltpu.SMEM)
        hbm = pl.BlockSpec(memory_space=pltpu.HBM)
        vmem = pl.BlockSpec(memory_space=pltpu.VMEM)
        f32 = jnp.float32
        dma = pltpu.SemaphoreType.DMA
        results = [
            jax.ShapeDtypeStruct((NK, NL), f32),
            jax.ShapeDtypeStruct((1, 1), f32),
            jax.ShapeDtypeStruct((NBLK, BLK), f32),
            jax.ShapeDtypeStruct((NBLK, BLK), f32),
        ]
        found = pl.pallas_call(
            lambda *refs: kernel(n_tm, n_region, *refs),
            out_shape=[pltpu.VMEM(leaf.shape, leaf.dtype) for leaf in results],
            in_specs=[hbm] * 5 + [smem, hbm, hbm, smem],
            out_specs=[vmem] * 4,
            scratch_shapes=[
                pltpu.VMEM((NBLK, BLK), f32),
                pltpu.SMEM(decays.shape, f32),
                pltpu.SMEM(widths.shape, f32),
                pltpu.VMEM(mix_start.shape, f32),
                pltpu.SMEM(pair_block.shape, jnp.int32),
                pltpu.SMEM(pair_source.shape, jnp.int32),
                pltpu.VMEM((CELL, 4, BLK), f32),
                pltpu.VMEM((1, BLK), jnp.int32),
                pltpu.VMEM((NEAR, 1, BLK), jnp.int32),
                pltpu.SMEM((NEAR, 1, BLK), jnp.int32),
                pltpu.VMEM((DEPTH - 1, PMAX, 4, BLK), f32),
                pltpu.VMEM((DEPTH, PMAX, 4, BLK), f32),
                pltpu.VMEM((PMAX, NL, 2, BLK, BLK), jnp.bfloat16),
                pltpu.VMEM((PMAX, NK * NL, BLK), f32),
                pltpu.VMEM((PMAX, NK, BLK), f32),
                pltpu.VMEM((PMAX, NK, BLK), f32),
                pltpu.VMEM((2, NL, BLK), f32),
                pltpu.VMEM((2 * ITERS, 4, BLK), f32),
                pltpu.VMEM((2 * ITERS, max(n_tm, n_region), 4, BLK), f32),
                pltpu.VMEM((NEAR + 1, 8, BLK), f32),
                dma((9,)),
                dma((NEAR,)),
                dma((NEAR,)),
                dma((2,)),
                dma((2,)),
                dma((DEPTH - 1,)),
                dma((DEPTH - 1,)),
                dma((NEAR,)),
                dma((NEAR,)),
                dma((2 * ITERS,)),
                dma((2 * ITERS,)),
            ],
            compiler_params=pltpu.CompilerParams(
                collective_id=0, has_side_effects=True, vmem_limit_bytes=60 * 2**20
            ),
            name="etas_em",
        )(
            blocks,
            jnp.reshape(background, (NBLK, BLK)),
            decays,
            widths,
            mix_start,
            rate_start,
            pair_block,
            pair_source,
            pair_count,
        )
        mixture, rate, share, offspring = pl.pallas_call(
            finish,
            out_shape=results,
            in_specs=[vmem] * 4,
            out_specs=[hbm] * 4,
            scratch_shapes=[dma((4,))],
            compiler_params=pltpu.CompilerParams(vmem_limit_bytes=2**20),
            name="hand_on",
        )(*found)
        return (
            mixture,
            jnp.reshape(rate, (1,)),
            jnp.reshape(share, (1, 1, NBLK * BLK)),
            jnp.reshape(offspring, (1, 1, NBLK * BLK)),
        )

    placed = (
        P("tm", "region", None, None),
        P("tm", "region", None),
        P(),
        P(),
        P(),
        P(),
        P("tm", "region", None),
        P("tm", "region", None),
        P("tm", "region"),
    )
    return jax.shard_map(
        body,
        mesh=mesh,
        in_specs=placed,
        out_specs=(P(), P(), P("tm", "region", None), P("tm", "region", None)),
        check_vma=False,
    )
```

```python
import math

import jax
import jax.numpy as jnp
from jax import lax
from jax.experimental import pallas as pl
from jax.experimental.pallas import tpu as pltpu
from jax.sharding import PartitionSpec as P

NK = 16
NL = 16
BLK = 128
NBLK = 24
DEPTH = 4
PMAX = 6
ITERS = 2
CELL = 3 * NBLK
NEAR = 3 * DEPTH - 1
PART = 80
RING = 8
FAR = 1.0e6
MESH = pl.DeviceIdType.MESH
PRODUCTIVITY = 1.0


def split_bf16(value):
    high = value.astype(jnp.bfloat16)
    low = (value - high.astype(jnp.float32)).astype(jnp.bfloat16)
    return high, low


def stacked_rows(value):
    high, low = split_bf16(value)
    return jnp.concatenate(
        [
            jnp.concatenate([high, high], axis=1),
            jnp.concatenate([low, jnp.zeros_like(low)], axis=1),
        ],
        axis=0,
    )


def spread_columns(ref, rows):
    for c in range(3):
        tile = jnp.concatenate([row[c : c + 1] for row in rows] + [rows[0][c : c + 1]] * (8 - len(rows)), axis=0)
        turned = jnp.transpose(tile)
        for p in range(len(rows)):
            ref[p, c] = jnp.broadcast_to(turned[:, p : p + 1], (BLK, BLK))


def columns(*rows):
    return jnp.transpose(jnp.concatenate(rows, axis=0))


def kernel(
    n_tm,
    n_region,
    ev_in,
    bg_in,
    decays_in,
    widths_in,
    mix_in,
    rate_s,
    block_in,
    source_in,
    count_s,
    mix_out,
    rate_out,
    share_out,
    offspring_out,
    bg_ref,
    decays_s,
    widths_s,
    mix_ref,
    block_s,
    source_s,
    events,
    beside,
    request,
    requests,
    cells,
    answer,
    picked,
    targets,
    sources,
    target_cols,
    source_cols,
    falloff,
    stats,
    early,
    late,
    coeff,
    payload_first,
    payload_last,
    partial_first,
    partial_last,
    returned,
    local_sem,
    request_send,
    request_recv,
    event_send,
    event_recv,
    answer_send,
    answer_recv,
    return_send,
    return_recv,
    sum_send,
    sum_recv,
):
    slab = lax.axis_index("tm")
    zone = lax.axis_index("region")
    events_all = float(n_tm * n_region * NBLK * BLK)
    payloads, partials = (payload_first, payload_last), (partial_first, partial_last)
    my_place = (zone, slab)

    def wrapped(place, step, length):
        moved = place + step
        return jnp.where(moved >= length, moved - length, jnp.where(moved < 0, moved + length, moved))

    def device(lag, side):
        return (wrapped(slab, lag, n_tm), wrapped(zone, side, n_region))

    x, z = lax.div(slab, RING), lax.div(zone, 2)
    y, core = slab - x * RING, zone - z * 2
    xs, zs = n_tm // RING, n_region // 2

    def hops(*steps):
        return -sum(min(step, length - step) for step, length in steps)

    row = sorted(
        ((dz, dc) for dz in range(zs) for dc in range(2) if dz or dc),
        key=lambda step: hops((step[0], zs)),
    )
    column = sorted(
        ((dx, dy) for dx in range(xs) for dy in range(RING) if dx or dy),
        key=lambda step: hops((step[0], xs), (step[1], RING)),
    )
    peers = (
        [(slab, wrapped(z, dz, zs) * 2 + wrapped(core, dc, 2)) for dz, dc in row],
        [(wrapped(x, dx, xs) * RING + wrapped(y, dy, RING), zone) for dx, dy in column],
    )

    staged = (
        (source_in, source_s),
        (block_in, block_s),
        (decays_in, decays_s),
        (widths_in, widths_s),
        (mix_in, mix_ref),
        (bg_in, bg_ref),
        (ev_in, events),
    )
    staging = [
        pltpu.make_async_copy(src, dst, local_sem.at[index])
        for index, (src, dst) in enumerate(staged)
    ]
    for copy in staging:
        copy.start()

    barrier = pltpu.get_barrier_semaphore()
    near = [(lag, 0) for lag in range(1, DEPTH)]
    near += [(lag, side) for lag in range(DEPTH) for side in (-1, 1)]
    greeted = [(-lag, side) for lag, side in near] + [(lag, -side) for lag, side in near if lag]
    greeted += [(0, step) for step in range(2, n_region - 1)]
    greeted += [(step, 0) for step in range(DEPTH, n_tm - DEPTH + 1)]
    for place in greeted:
        pl.semaphore_signal(barrier, inc=1, device_id=device(*place), device_id_type=MESH)
    staging[0].wait()
    row8 = lax.broadcasted_iota(jnp.int32, (8, BLK), 0)
    asked = jnp.zeros((8, BLK), jnp.int32)
    for p in range(PMAX):
        asked = jnp.where(row8 == p, source_s[0, 0, p], asked)
    request[...] = asked
    pl.semaphore_wait(barrier, len(greeted))

    pending = []

    def send(src, dst, send_sem, recv_sem, device):
        copy = pltpu.make_async_remote_copy(
            src_ref=src,
            dst_ref=dst,
            send_sem=send_sem,
            recv_sem=recv_sem,
            device_id=device,
            device_id_type=MESH,
        )
        copy.start()
        pending.append(copy)
        return copy

    def ask(index):
        lag, side = near[index]
        return send(
            request,
            requests.at[index],
            request_send.at[index],
            request_recv.at[index],
            device(-lag, side),
        )

    askers = DEPTH - 1
    request_copies = [ask(index) for index in range(askers)]

    staging[-1].wait()
    event_copies = [
        send(
            events,
            beside.at[side],
            event_send.at[side],
            event_recv.at[side],
            device(0, 1 - 2 * side),
        )
        for side in range(2)
    ]
    for copy in staging[1:-1]:
        copy.wait()
    decay_col = jnp.zeros((NK, BLK), jnp.float32)
    row16 = lax.broadcasted_iota(jnp.int32, (NK, BLK), 0)
    for k in range(NK):
        decay_col = jnp.where(row16 == k, decays_s[k], decay_col)
    width_col = jnp.zeros((NL, BLK), jnp.float32)
    for l in range(NL):
        width_col = jnp.where(row16 == l, widths_s[l], width_col)
    spread = 2.0 * width_col * width_col
    coeff[0] = -math.log2(math.e) / spread
    coeff[1] = 1.0 / (math.pi * spread)
    mix_tile = mix_ref[...]
    mixture = [jnp.broadcast_to(mix_tile[:, l : l + 1], (NK, BLK)) for l in range(NL)]
    mixture = jnp.concatenate(mixture, axis=0)
    own_yield = jnp.sum(jnp.exp(PRODUCTIVITY * events[:, 3, :]), axis=0, keepdims=True)
    own_yield = jnp.broadcast_to(jnp.sum(own_yield, axis=1, keepdims=True), (1, BLK))

    start_time = slab.astype(jnp.float32)
    live_count = count_s[0, 0]
    own_targets = [events[block_s[0, 0, p]] for p in range(PMAX)]
    for p, rows in enumerate(own_targets):
        targets[p] = rows
        live = jnp.where(p < live_count, 1.0, 0.0)
        late[p] = decay_col * jnp.exp(-decay_col * (rows[0:1] - start_time)) * live
    spread_columns(target_cols, own_targets)

    lane = lax.broadcasted_iota(jnp.int32, (8, 2 * BLK), 1)
    cell = jnp.where(lane >= 2 * PART, lane - 2 * PART, jnp.where(lane >= PART, lane - PART, lane))
    cell = jnp.where(lane >= 3 * PART, -1, cell)

    def one_hot(tile, lag):
        named = jnp.concatenate([tile, tile], axis=1) - lag * CELL
        return jnp.where(named == cell, 1.0, 0.0)

    for copy in event_copies:
        copy.wait_recv()
    for c in range(4):
        value = jnp.concatenate(
            [
                beside[0, :, c, :],
                events[:, c, :],
                beside[1, :, c, :],
                jnp.zeros((PART - CELL, BLK), jnp.float32),
            ],
            axis=0,
        )
        at = slice(c * BLK, (c + 1) * BLK)
        for part in range(3):
            term = value.astype(jnp.bfloat16)
            cells[part * PART : (part + 1) * PART, at] = term
            value = value - term.astype(jnp.float32)
        cells[3 * PART :, at] = jnp.zeros((2 * BLK - 3 * PART, BLK), jnp.bfloat16)
    for copy in request_copies:
        copy.wait_recv()
    wanted = [one_hot(asked, 0)] + [one_hot(requests[lag - 1], lag) for lag in range(1, DEPTH)]
    wanted = jnp.concatenate(wanted, axis=0).astype(jnp.bfloat16)
    found = jnp.dot(wanted, cells[...], preferred_element_type=jnp.float32)
    answer_copies = []
    for lag in range(DEPTH - 1, -1, -1):
        place = picked.at[0] if lag == 0 else answer.at[lag - 1]
        for c in range(4):
            place[c] = found[8 * lag : 8 * lag + 8, c * BLK : (c + 1) * BLK]
        if lag:
            answer_copies.append(
                send(
                    place,
                    picked.at[lag],
                    answer_send.at[lag - 1],
                    answer_recv.at[lag - 1],
                    device(lag, 0),
                )
            )
    for copy in answer_copies:
        copy.wait_recv()
    chosen = []
    for c in range(4):
        tile = picked[0, c]
        for lag in range(1, DEPTH):
            tile = jnp.where(asked >= lag * CELL, picked[lag, c], tile)
        chosen.append(tile)
    own_sources = [
        jnp.concatenate([chosen[c][p : p + 1] for c in range(4)], axis=0) for p in range(PMAX)
    ]
    for p, rows in enumerate(own_sources):
        sources[p] = rows
        early[p] = jnp.exp(decay_col * (rows[0:1] - start_time)) * jnp.exp(PRODUCTIVITY * rows[3:4])
    for c in range(3):
        turned = jnp.transpose(chosen[c])
        for p in range(PMAX):
            source_cols[p, c] = jnp.broadcast_to(turned[:, p : p + 1], (BLK, BLK))

    def distances(target, source):
        gap_time = target[0] - source[0]
        gap_east = target[1] - source[1]
        gap_north = target[2] - source[2]
        square = gap_east * gap_east + gap_north * gap_north
        return jnp.where(gap_time > 0.0, square, FAR)

    def as_rows(value):
        return [value[c : c + 1] for c in range(3)]

    def fall(square, l):
        return split_bf16(jnp.exp2(square * coeff[0, l : l + 1, :]))

    def prepare(index, carry):
        for p in (2 * index, 2 * index + 1):
            after = late[p]
            left = stacked_rows(early[p])
            square = distances(as_rows(targets[p]), [source_cols[p, c] for c in range(3)])
            for pair in range(NL // 2):
                parts = [
                    jnp.concatenate(fall(square, l), axis=0) for l in (2 * pair, 2 * pair + 1)
                ]
                right = jnp.concatenate(parts, axis=1)
                both = jnp.dot(left, right, preferred_element_type=jnp.float32)
                both = both[:NK] + both[NK:]
                for side in range(2):
                    l = 2 * pair + side
                    stats[p, l * NK : (l + 1) * NK, :] = (
                        both[:, side * BLK : (side + 1) * BLK] * after * coeff[1, l : l + 1, :]
                    )
        return carry

    lax.fori_loop(0, PMAX // 2, prepare, 0)

    def prepare_back(index, carry):
        for p in (2 * index, 2 * index + 1):
            square = distances([target_cols[p, c] for c in range(3)], as_rows(sources[p]))
            for l in range(NL):
                falloff[p, l, 0], falloff[p, l, 1] = fall(square, l)
        return carry

    block_row = lax.broadcasted_iota(jnp.int32, (NBLK, BLK), 0)
    background = bg_ref[...]

    def expect(mixture, rate):
        triggered = jnp.zeros((NBLK, BLK), jnp.float32)
        for p in range(PMAX):
            row = jnp.sum(stats[p] * mixture, axis=0, keepdims=True)
            triggered = triggered + jnp.where(block_row == block_s[0, 0, p], row, 0.0)
        level = rate * background
        inverse = 1.0 / (level + triggered)
        share = level * inverse
        weights = [
            jnp.sum(jnp.where(block_row == block_s[0, 0, p], inverse, 0.0), axis=0, keepdims=True)
            for p in range(PMAX)
        ]
        scores = stats[0] * weights[0]
        for p in range(1, PMAX):
            scores = scores + stats[p] * weights[p]
        rows = [
            jnp.sum(jnp.transpose(scores[half * BLK : (half + 1) * BLK]), axis=0, keepdims=True)
            for half in range(2)
        ]
        return share, weights, rows

    def start_sum(stage, value):
        sweep, axis = divmod(stage, 2)
        payload, partial = payloads[sweep].at[axis], partials[sweep].at[axis]
        payload[...] = value
        partial[my_place[axis]] = value
        for other in peers[axis]:
            pltpu.make_async_remote_copy(
                src_ref=payload,
                dst_ref=partial.at[my_place[axis]],
                send_sem=sum_send.at[stage],
                recv_sem=sum_recv.at[stage],
                device_id=other,
                device_id_type=MESH,
            ).start()

    def others(stage, sems):
        sweep, axis = divmod(stage, 2)
        part = partials[sweep].at[axis, pl.ds(0, len(peers[axis]))]
        return pltpu.make_async_copy(part, part, sems.at[stage])

    def end_sum(stage):
        sweep, axis = divmod(stage, 2)
        others(stage, sum_recv).wait()
        return jnp.sum(partials[sweep][axis, 0 : len(peers[axis]) + 1], axis=0)

    def update(mixture, total, yield_total):
        cols = columns(*([total] * (8 // total.shape[0])))
        factor = jnp.concatenate(
            [jnp.broadcast_to(cols[:, half : half + 1], (BLK, BLK)) for half in range(2)], axis=0
        )
        mass = mixture * factor
        triggered = jnp.sum(mass, axis=0, keepdims=True)
        return mass / yield_total, 1.0 - triggered / events_all

    share, weights, rows = expect(mixture, jnp.full((1, BLK), rate_s[0], jnp.float32))
    value = jnp.concatenate(rows + [own_yield, own_yield], axis=0)
    start_sum(0, value)
    request_copies = [ask(index) for index in range(askers, len(near))]
    lax.fori_loop(0, 2, prepare_back, 0)
    value = end_sum(0)
    start_sum(1, value)
    lax.fori_loop(2, 3, prepare_back, 0)
    for copy in request_copies:
        copy.wait_recv()
    for copy in pending:
        copy.wait_send()
    pending.clear()
    value = end_sum(1)
    yield_total = value[2:3, :]
    mixture, rate = update(mixture, value, yield_total)

    share, weights, rows = expect(mixture, rate)
    start_sum(2, jnp.concatenate(rows, axis=0))
    share_out[...] = share
    scaled = mixture * jnp.concatenate(
        [jnp.broadcast_to(coeff[1, l : l + 1, :], (NK, BLK)) for l in range(NL)], axis=0
    )

    for p in range(PMAX):
        late[p] = late[p] * weights[p]

    stats[0] = scaled

    def give_back(index, rows):
        for p in (2 * index, 2 * index + 1):
            left = stacked_rows(late[p])
            gathered = jnp.zeros((NK, BLK), jnp.float32)
            for pair in range(NL // 2):
                right = jnp.concatenate(
                    [
                        jnp.concatenate([falloff[p, l, 0], falloff[p, l, 1]], axis=0)
                        for l in (2 * pair, 2 * pair + 1)
                    ],
                    axis=1,
                )
                both = jnp.dot(left, right, preferred_element_type=jnp.float32)
                both = both[:NK] + both[NK:]
                for side in range(2):
                    l = 2 * pair + side
                    gathered = (
                        gathered
                        + both[:, side * BLK : (side + 1) * BLK] * stats[0, l * NK : (l + 1) * NK, :]
                    )
            row = jnp.sum(gathered * early[p], axis=0, keepdims=True)
            rows = jnp.where(lax.broadcasted_iota(jnp.int32, (8, BLK), 0) == p, row, rows)
        return rows

    rows = lax.fori_loop(0, PMAX // 2, give_back, jnp.zeros((8, BLK), jnp.float32))
    returned[0] = rows
    return_copies = [
        send(
            returned.at[0],
            returned.at[index + 1],
            return_send.at[index],
            return_recv.at[index],
            device(-lag, side),
        )
        for index, (lag, side) in enumerate(near)
    ]
    value = end_sum(2)
    start_sum(3, value)

    for copy in return_copies:
        copy.wait_recv()
    gathered = jnp.zeros((NBLK, BLK), jnp.float32)
    for index, (lag, side) in enumerate([(0, 0)] + near):
        first = (lag * 3 + side + 1) * NBLK
        for p in range(PMAX):
            named = asked[p : p + 1] if index == 0 else requests[index - 1, p : p + 1, :]
            gathered = gathered + jnp.where(
                block_row == named - first, returned[index, p : p + 1, :], 0.0
            )
    offspring_out[...] = gathered
    for copy in pending:
        copy.wait_send()
    for stage in range(3):
        others(stage, sum_send).wait()
    value = end_sum(3)
    others(3, sum_send).wait()
    mixture, rate = update(mixture, value, yield_total)
    lane16 = lax.broadcasted_iota(jnp.int32, (NK, BLK), 1)
    square_mix = jnp.zeros((NK, BLK), jnp.float32)
    for l in range(NL):
        square_mix = jnp.where(lane16 == l, mixture[l * NK : (l + 1) * NK], square_mix)
    mix_out[...] = square_mix[:, :NL]
    rate_out[...] = rate[:, 0:1]


def finish(*refs):
    arrived, handed, sems = refs[:4], refs[4:8], refs[8]
    copies = [
        pltpu.make_async_copy(src, dst, sems.at[index])
        for index, (src, dst) in enumerate(zip(arrived, handed))
    ]
    for copy in copies:
        copy.start()
    for copy in copies:
        copy.wait()


def solution(mesh):
    n_tm, n_region = mesh.shape["tm"], mesh.shape["region"]

    def body(
        events, background, decays, widths, mix_start, rate_start, pair_block, pair_source, pair_count
    ):
        blocks = jnp.transpose(jnp.reshape(events, (4, NBLK, BLK)), (1, 0, 2))
        smem = pl.BlockSpec(memory_space=pltpu.SMEM)
        hbm = pl.BlockSpec(memory_space=pltpu.HBM)
        vmem = pl.BlockSpec(memory_space=pltpu.VMEM)
        f32 = jnp.float32
        dma = pltpu.SemaphoreType.DMA
        results = [
            jax.ShapeDtypeStruct((NK, NL), f32),
            jax.ShapeDtypeStruct((1, 1), f32),
            jax.ShapeDtypeStruct((NBLK, BLK), f32),
            jax.ShapeDtypeStruct((NBLK, BLK), f32),
        ]
        found = pl.pallas_call(
            lambda *refs: kernel(n_tm, n_region, *refs),
            out_shape=[pltpu.VMEM(leaf.shape, leaf.dtype) for leaf in results],
            in_specs=[hbm] * 5 + [smem, hbm, hbm, smem],
            out_specs=[vmem] * 4,
            scratch_shapes=[
                pltpu.VMEM((NBLK, BLK), f32),
                pltpu.SMEM(decays.shape, f32),
                pltpu.SMEM(widths.shape, f32),
                pltpu.VMEM(mix_start.shape, f32),
                pltpu.SMEM(pair_block.shape, jnp.int32),
                pltpu.SMEM(pair_source.shape, jnp.int32),
                pltpu.VMEM((NBLK, 4, BLK), f32),
                pltpu.VMEM((2, NBLK, 4, BLK), f32),
                pltpu.VMEM((8, BLK), jnp.int32),
                pltpu.VMEM((NEAR, 8, BLK), jnp.int32),
                pltpu.VMEM((2 * BLK, 4 * BLK), jnp.bfloat16),
                pltpu.VMEM((DEPTH - 1, 4, 8, BLK), f32),
                pltpu.VMEM((DEPTH, 4, 8, BLK), f32),
                pltpu.VMEM((PMAX, 4, BLK), f32),
                pltpu.VMEM((PMAX, 4, BLK), f32),
                pltpu.VMEM((PMAX, 3, BLK, BLK), f32),
                pltpu.VMEM((PMAX, 3, BLK, BLK), f32),
                pltpu.VMEM((PMAX, NL, 2, BLK, BLK), jnp.bfloat16),
                pltpu.VMEM((PMAX, NK * NL, BLK), f32),
                pltpu.VMEM((PMAX, NK, BLK), f32),
                pltpu.VMEM((PMAX, NK, BLK), f32),
                pltpu.VMEM((2, NL, BLK), f32),
                pltpu.VMEM((2, 4, BLK), f32),
                pltpu.VMEM((2, 2, BLK), f32),
                pltpu.VMEM((2, max(n_tm, n_region), 4, BLK), f32),
                pltpu.VMEM((2, max(n_tm, n_region), 2, BLK), f32),
                pltpu.VMEM((NEAR + 1, 8, BLK), f32),
                dma((7,)),
                dma((NEAR,)),
                dma((NEAR,)),
                dma((2,)),
                dma((2,)),
                dma((DEPTH - 1,)),
                dma((DEPTH - 1,)),
                dma((NEAR,)),
                dma((NEAR,)),
                dma((2 * ITERS,)),
                dma((2 * ITERS,)),
            ],
            compiler_params=pltpu.CompilerParams(
                collective_id=0, has_side_effects=True, vmem_limit_bytes=60 * 2**20
            ),
            name="etas_em",
        )(
            blocks,
            jnp.reshape(background, (NBLK, BLK)),
            decays,
            widths,
            mix_start,
            rate_start,
            pair_block,
            pair_source,
            pair_count,
        )
        mixture, rate, share, offspring = pl.pallas_call(
            finish,
            out_shape=results,
            in_specs=[vmem] * 4,
            out_specs=[hbm] * 4,
            scratch_shapes=[dma((4,))],
            compiler_params=pltpu.CompilerParams(vmem_limit_bytes=2**20),
            name="hand_on",
        )(*found)
        return (
            mixture,
            jnp.reshape(rate, (1,)),
            jnp.reshape(share, (1, 1, NBLK * BLK)),
            jnp.reshape(offspring, (1, 1, NBLK * BLK)),
        )

    placed = (
        P("tm", "region", None, None),
        P("tm", "region", None),
        P(),
        P(),
        P(),
        P(),
        P("tm", "region", None),
        P("tm", "region", None),
        P("tm", "region"),
    )
    return jax.shard_map(
        body,
        mesh=mesh,
        in_specs=placed,
        out_specs=(P(), P(), P("tm", "region", None), P("tm", "region", None)),
        check_vma=False,
    )
```

```python
import math

import jax
import jax.numpy as jnp
from jax import lax
from jax.experimental import pallas as pl
from jax.experimental.pallas import tpu as pltpu
from jax.sharding import PartitionSpec as P

NK = 16
NL = 16
BLK = 128
NBLK = 24
DEPTH = 4
PMAX = 6
ITERS = 2
CELL = 3 * NBLK
NEAR = 3 * DEPTH - 1
PART = 80
RING = 8
FAR = 1.0e6
MESH = pl.DeviceIdType.MESH
PRODUCTIVITY = 1.0


def split_bf16(value):
    high = value.astype(jnp.bfloat16)
    low = (value - high.astype(jnp.float32)).astype(jnp.bfloat16)
    return high, low


def stacked_rows(value):
    high, low = split_bf16(value)
    return jnp.concatenate(
        [
            jnp.concatenate([high, high], axis=1),
            jnp.concatenate([low, jnp.zeros_like(low)], axis=1),
        ],
        axis=0,
    )


def spread_columns(ref, rows):
    for c in range(3):
        tile = jnp.concatenate([row[c : c + 1] for row in rows] + [rows[0][c : c + 1]] * (8 - len(rows)), axis=0)
        turned = jnp.transpose(tile)
        for p in range(len(rows)):
            ref[p, c] = jnp.broadcast_to(turned[:, p : p + 1], (BLK, BLK))


def columns(*rows):
    return jnp.transpose(jnp.concatenate(rows, axis=0))


def kernel(
    n_tm,
    n_region,
    ev_in,
    bg_in,
    decays_in,
    widths_in,
    mix_in,
    rate_s,
    block_in,
    source_in,
    count_s,
    mix_out,
    rate_out,
    share_out,
    offspring_out,
    bg_ref,
    decays_s,
    widths_s,
    mix_ref,
    block_s,
    source_s,
    events,
    beside,
    request,
    requests,
    cells,
    answer,
    picked,
    targets,
    sources,
    target_cols,
    falloff,
    stats,
    early,
    late,
    coeff,
    payload_first,
    payload_last,
    partial_first,
    partial_last,
    returned,
    local_sem,
    request_send,
    request_recv,
    event_send,
    event_recv,
    answer_send,
    answer_recv,
    return_send,
    return_recv,
    sum_send,
    sum_recv,
):
    slab = lax.axis_index("tm")
    zone = lax.axis_index("region")
    events_all = float(n_tm * n_region * NBLK * BLK)
    payloads, partials = (payload_first, payload_last), (partial_first, partial_last)

    def wrapped(place, step, length):
        moved = place + step
        return jnp.where(moved >= length, moved - length, jnp.where(moved < 0, moved + length, moved))

    def device(lag, side):
        return (wrapped(slab, lag, n_tm), wrapped(zone, side, n_region))

    x, z = lax.div(slab, RING), lax.div(zone, 2)
    y, core = slab - x * RING, zone - z * 2
    xs, zs = n_tm // RING, n_region // 2

    def hops(*steps):
        return -sum(min(step, length - step) for step, length in steps)

    row = sorted(
        ((dy, dc) for dy in range(RING) for dc in range(2) if dy or dc),
        key=lambda step: hops((step[0], RING)),
    )
    column = sorted(
        ((dx, dz) for dx in range(xs) for dz in range(zs) if dx or dz),
        key=lambda step: hops((step[0], xs), (step[1], zs)),
    )
    peers = (
        [(x * RING + wrapped(y, dy, RING), z * 2 + wrapped(core, dc, 2)) for dy, dc in row],
        [(wrapped(x, dx, xs) * RING + y, wrapped(z, dz, zs) * 2 + core) for dx, dz in column],
    )
    my_place = (y * 2 + core, x * zs + z)

    staged = (
        (source_in, source_s),
        (block_in, block_s),
        (decays_in, decays_s),
        (widths_in, widths_s),
        (mix_in, mix_ref),
        (bg_in, bg_ref),
        (ev_in, events),
    )
    staging = [
        pltpu.make_async_copy(src, dst, local_sem.at[index])
        for index, (src, dst) in enumerate(staged)
    ]
    for copy in staging:
        copy.start()

    barrier = pltpu.get_barrier_semaphore()
    near = [(lag, 0) for lag in range(1, DEPTH)]
    near += [(lag, side) for lag in range(DEPTH) for side in (-1, 1)]
    greeted = [
        (hops((step[0], RING)), place) for step, place in zip(row, peers[0])
    ] + [
        (hops((step[0], xs), (step[1], zs)), place) for step, place in zip(column, peers[1])
    ]
    for lag, side in near:
        greeted.append((-lag - abs(side), device(-lag, side)))
        if lag:
            greeted.append((-lag - abs(side), device(lag, -side)))
    for _, place in sorted(greeted, key=lambda entry: entry[0]):
        pl.semaphore_signal(barrier, inc=1, device_id=place, device_id_type=MESH)
    staging[0].wait()
    row8 = lax.broadcasted_iota(jnp.int32, (8, BLK), 0)
    asked = jnp.zeros((8, BLK), jnp.int32)
    for p in range(PMAX):
        asked = jnp.where(row8 == p, source_s[0, 0, p], asked)
    request[...] = asked
    pl.semaphore_wait(barrier, len(greeted))

    pending = []

    def send(src, dst, send_sem, recv_sem, device):
        copy = pltpu.make_async_remote_copy(
            src_ref=src,
            dst_ref=dst,
            send_sem=send_sem,
            recv_sem=recv_sem,
            device_id=device,
            device_id_type=MESH,
        )
        copy.start()
        pending.append(copy)
        return copy

    def ask(index):
        lag, side = near[index]
        return send(
            request,
            requests.at[index],
            request_send.at[index],
            request_recv.at[index],
            device(-lag, side),
        )

    askers = DEPTH - 1
    request_copies = [ask(index) for index in range(askers)]

    staging[-1].wait()
    event_copies = [
        send(
            events,
            beside.at[side],
            event_send.at[side],
            event_recv.at[side],
            device(0, 1 - 2 * side),
        )
        for side in range(2)
    ]
    for copy in staging[1:-1]:
        copy.wait()
    decay_col = jnp.zeros((NK, BLK), jnp.float32)
    row16 = lax.broadcasted_iota(jnp.int32, (NK, BLK), 0)
    for k in range(NK):
        decay_col = jnp.where(row16 == k, decays_s[k], decay_col)
    width_col = jnp.zeros((NL, BLK), jnp.float32)
    for l in range(NL):
        width_col = jnp.where(row16 == l, widths_s[l], width_col)
    spread = 2.0 * width_col * width_col
    coeff[0] = -math.log2(math.e) / spread
    coeff[1] = 1.0 / (math.pi * spread)
    mix_tile = mix_ref[...]
    mixture = [jnp.broadcast_to(mix_tile[:, l : l + 1], (NK, BLK)) for l in range(NL)]
    mixture = jnp.concatenate(mixture, axis=0)
    own_yield = jnp.sum(jnp.exp(PRODUCTIVITY * events[:, 3, :]), axis=0, keepdims=True)
    own_yield = jnp.broadcast_to(jnp.sum(own_yield, axis=1, keepdims=True), (1, BLK))

    start_time = slab.astype(jnp.float32)
    live_count = count_s[0, 0]
    own_targets = [events[block_s[0, 0, p]] for p in range(PMAX)]
    for p, rows in enumerate(own_targets):
        targets[p] = rows
        live = jnp.where(p < live_count, 1.0, 0.0)
        late[p] = decay_col * jnp.exp(-decay_col * (rows[0:1] - start_time)) * live
    spread_columns(target_cols, own_targets)

    lane = lax.broadcasted_iota(jnp.int32, (8, 2 * BLK), 1)
    cell = jnp.where(lane >= 2 * PART, lane - 2 * PART, jnp.where(lane >= PART, lane - PART, lane))
    cell = jnp.where(lane >= 3 * PART, -1, cell)

    def one_hot(tile, lag):
        named = jnp.concatenate([tile, tile], axis=1) - lag * CELL
        return jnp.where(named == cell, 1.0, 0.0)

    for copy in event_copies:
        copy.wait_recv()
    for c in range(4):
        value = jnp.concatenate(
            [
                beside[0, :, c, :],
                events[:, c, :],
                beside[1, :, c, :],
                jnp.zeros((PART - CELL, BLK), jnp.float32),
            ],
            axis=0,
        )
        at = slice(c * BLK, (c + 1) * BLK)
        for part in range(3):
            term = value.astype(jnp.bfloat16)
            cells[part * PART : (part + 1) * PART, at] = term
            value = value - term.astype(jnp.float32)
        cells[3 * PART :, at] = jnp.zeros((2 * BLK - 3 * PART, BLK), jnp.bfloat16)
    for copy in request_copies:
        copy.wait_recv()
    wanted = [one_hot(asked, 0)] + [one_hot(requests[lag - 1], lag) for lag in range(1, DEPTH)]
    wanted = jnp.concatenate(wanted, axis=0).astype(jnp.bfloat16)
    found = jnp.dot(wanted, cells[...], preferred_element_type=jnp.float32)
    answer_copies = []
    for lag in range(DEPTH - 1, -1, -1):
        place = picked.at[0] if lag == 0 else answer.at[lag - 1]
        place[...] = jnp.concatenate(
            [found[8 * lag : 8 * lag + PMAX, c * BLK : (c + 1) * BLK] for c in range(4)], axis=0
        )
        if lag:
            answer_copies.append(
                send(
                    place,
                    picked.at[lag],
                    answer_send.at[lag - 1],
                    answer_recv.at[lag - 1],
                    device(lag, 0),
                )
            )
    asked_rows = jnp.concatenate([asked[:PMAX]] * 4, axis=0)
    for copy in answer_copies:
        copy.wait_recv()
    chosen = picked[0]
    for lag in range(1, DEPTH):
        chosen = jnp.where(asked_rows >= lag * CELL, picked[lag], chosen)
    turned = jnp.transpose(chosen)
    for p in range(PMAX):
        rows = [chosen[c * PMAX + p : c * PMAX + p + 1] for c in range(4)]
        sources[p] = jnp.concatenate(rows, axis=0)
        early[p] = jnp.exp(decay_col * (rows[0] - start_time)) * jnp.exp(PRODUCTIVITY * rows[3])

    def distances(target, source):
        gap_time = target[0] - source[0]
        gap_east = target[1] - source[1]
        gap_north = target[2] - source[2]
        square = gap_east * gap_east + gap_north * gap_north
        return jnp.where(gap_time > 0.0, square, FAR)

    def as_rows(value):
        return [value[c : c + 1] for c in range(3)]

    def fall(square, l):
        return split_bf16(jnp.exp2(square * coeff[0, l : l + 1, :]))

    first_rows = []
    for p in range(PMAX):
        after = late[p]
        left = stacked_rows(early[p])
        square = distances(
            as_rows(targets[p]),
            [turned[:, c * PMAX + p : c * PMAX + p + 1] for c in range(3)],
        )
        summed = jnp.zeros((NK, BLK), jnp.float32)
        for pair in range(NL // 2):
            parts = [jnp.concatenate(fall(square, l), axis=0) for l in (2 * pair, 2 * pair + 1)]
            right = jnp.concatenate(parts, axis=1)
            both = jnp.dot(left, right, preferred_element_type=jnp.float32)
            both = both[:NK] + both[NK:]
            for side in range(2):
                l = 2 * pair + side
                tile = both[:, side * BLK : (side + 1) * BLK] * after * coeff[1, l : l + 1, :]
                stats[p, l * NK : (l + 1) * NK, :] = tile
                summed = summed + tile * mixture[l * NK : (l + 1) * NK]
        first_rows.append(jnp.sum(summed, axis=0, keepdims=True))

    def prepare_back(index, carry):
        for p in (2 * index, 2 * index + 1):
            square = distances([target_cols[p, c] for c in range(3)], as_rows(sources[p]))
            for l in range(NL):
                falloff[p, l, 0], falloff[p, l, 1] = fall(square, l)
        return carry

    block_row = lax.broadcasted_iota(jnp.int32, (NBLK, BLK), 0)
    background = bg_ref[...]

    def expect(row_of, rate):
        triggered = jnp.zeros((NBLK, BLK), jnp.float32)
        for p in range(PMAX):
            row = row_of(p)
            triggered = triggered + jnp.where(block_row == block_s[0, 0, p], row, 0.0)
        level = rate * background
        inverse = 1.0 / (level + triggered)
        share = level * inverse
        weights = [
            jnp.sum(jnp.where(block_row == block_s[0, 0, p], inverse, 0.0), axis=0, keepdims=True)
            for p in range(PMAX)
        ]
        scores = stats[0] * weights[0]
        for p in range(1, PMAX):
            scores = scores + stats[p] * weights[p]
        rows = [
            jnp.sum(jnp.transpose(scores[half * BLK : (half + 1) * BLK]), axis=0, keepdims=True)
            for half in range(2)
        ]
        return share, weights, rows

    def start_sum(stage, value):
        sweep, axis = divmod(stage, 2)
        payload, partial = payloads[sweep].at[axis], partials[sweep].at[axis]
        payload[...] = value
        partial[my_place[axis]] = value
        for other in peers[axis]:
            pltpu.make_async_remote_copy(
                src_ref=payload,
                dst_ref=partial.at[my_place[axis]],
                send_sem=sum_send.at[stage],
                recv_sem=sum_recv.at[stage],
                device_id=other,
                device_id_type=MESH,
            ).start()

    def others(stage, sems):
        sweep, axis = divmod(stage, 2)
        part = partials[sweep].at[axis, pl.ds(0, len(peers[axis]))]
        return pltpu.make_async_copy(part, part, sems.at[stage])

    def end_sum(stage):
        sweep, axis = divmod(stage, 2)
        others(stage, sum_recv).wait()
        return jnp.sum(partials[sweep][axis, 0 : len(peers[axis]) + 1], axis=0)

    def update(mixture, total, yield_total):
        cols = columns(*([total] * (8 // total.shape[0])))
        factor = jnp.concatenate(
            [jnp.broadcast_to(cols[:, half : half + 1], (BLK, BLK)) for half in range(2)], axis=0
        )
        mass = mixture * factor
        triggered = jnp.sum(mass, axis=0, keepdims=True)
        return mass * (1.0 / yield_total), 1.0 - triggered / events_all

    share, weights, rows = expect(lambda p: first_rows[p], jnp.full((1, BLK), rate_s[0], jnp.float32))
    value = jnp.concatenate(rows + [own_yield, own_yield], axis=0)
    start_sum(0, value)
    request_copies = [ask(index) for index in range(askers, len(near))]
    lax.fori_loop(0, 2, prepare_back, 0)
    value = end_sum(0)
    start_sum(1, value)
    lax.fori_loop(2, 3, prepare_back, 0)
    for copy in request_copies:
        copy.wait_recv()
    for copy in pending:
        copy.wait_send()
    pending.clear()
    value = end_sum(1)
    yield_total = value[2:3, :]
    mixture, rate = update(mixture, value, yield_total)

    share, weights, rows = expect(
        lambda p: jnp.sum(stats[p] * mixture, axis=0, keepdims=True), rate
    )
    start_sum(2, jnp.concatenate(rows, axis=0))
    share_out[...] = share
    scaled = mixture * jnp.concatenate(
        [jnp.broadcast_to(coeff[1, l : l + 1, :], (NK, BLK)) for l in range(NL)], axis=0
    )

    for p in range(PMAX):
        late[p] = late[p] * weights[p]

    stats[0] = scaled

    def give_back(index, rows):
        for p in (2 * index, 2 * index + 1):
            left = stacked_rows(late[p])
            gathered = jnp.zeros((NK, BLK), jnp.float32)
            for pair in range(NL // 2):
                right = jnp.concatenate(
                    [
                        jnp.concatenate([falloff[p, l, 0], falloff[p, l, 1]], axis=0)
                        for l in (2 * pair, 2 * pair + 1)
                    ],
                    axis=1,
                )
                both = jnp.dot(left, right, preferred_element_type=jnp.float32)
                both = both[:NK] + both[NK:]
                for side in range(2):
                    l = 2 * pair + side
                    gathered = (
                        gathered
                        + both[:, side * BLK : (side + 1) * BLK] * stats[0, l * NK : (l + 1) * NK, :]
                    )
            row = jnp.sum(gathered * early[p], axis=0, keepdims=True)
            rows = jnp.where(lax.broadcasted_iota(jnp.int32, (8, BLK), 0) == p, row, rows)
        return rows

    rows = lax.fori_loop(0, PMAX // 2, give_back, jnp.zeros((8, BLK), jnp.float32))
    returned[0] = rows
    return_copies = [
        send(
            returned.at[0],
            returned.at[index + 1],
            return_send.at[index],
            return_recv.at[index],
            device(-lag, side),
        )
        for index, (lag, side) in enumerate(near)
    ]
    value = end_sum(2)
    start_sum(3, value)

    for copy in return_copies:
        copy.wait_recv()
    gathered = jnp.zeros((NBLK, BLK), jnp.float32)
    for index, (lag, side) in enumerate([(0, 0)] + near):
        first = (lag * 3 + side + 1) * NBLK
        for p in range(PMAX):
            named = asked[p : p + 1] if index == 0 else requests[index - 1, p : p + 1, :]
            gathered = gathered + jnp.where(
                block_row == named - first, returned[index, p : p + 1, :], 0.0
            )
    offspring_out[...] = gathered
    for copy in pending:
        copy.wait_send()
    for stage in range(3):
        others(stage, sum_send).wait()
    value = end_sum(3)
    others(3, sum_send).wait()
    mixture, rate = update(mixture, value, yield_total)
    lane16 = lax.broadcasted_iota(jnp.int32, (NK, BLK), 1)
    square_mix = jnp.zeros((NK, BLK), jnp.float32)
    for l in range(NL):
        square_mix = jnp.where(lane16 == l, mixture[l * NK : (l + 1) * NK], square_mix)
    mix_out[...] = square_mix[:, :NL]
    rate_out[...] = rate[:, 0:1]


def finish(*refs):
    arrived, handed, sems = refs[:4], refs[4:8], refs[8]
    copies = [
        pltpu.make_async_copy(src, dst, sems.at[index])
        for index, (src, dst) in enumerate(zip(arrived, handed))
    ]
    for copy in copies:
        copy.start()
    for copy in copies:
        copy.wait()


def solution(mesh):
    n_tm, n_region = mesh.shape["tm"], mesh.shape["region"]

    def body(
        events, background, decays, widths, mix_start, rate_start, pair_block, pair_source, pair_count
    ):
        blocks = jnp.transpose(jnp.reshape(events, (4, NBLK, BLK)), (1, 0, 2))
        smem = pl.BlockSpec(memory_space=pltpu.SMEM)
        hbm = pl.BlockSpec(memory_space=pltpu.HBM)
        vmem = pl.BlockSpec(memory_space=pltpu.VMEM)
        f32 = jnp.float32
        dma = pltpu.SemaphoreType.DMA
        results = [
            jax.ShapeDtypeStruct((NK, NL), f32),
            jax.ShapeDtypeStruct((1, 1), f32),
            jax.ShapeDtypeStruct((NBLK, BLK), f32),
            jax.ShapeDtypeStruct((NBLK, BLK), f32),
        ]
        found = pl.pallas_call(
            lambda *refs: kernel(n_tm, n_region, *refs),
            out_shape=[pltpu.VMEM(leaf.shape, leaf.dtype) for leaf in results],
            in_specs=[hbm] * 5 + [smem, hbm, hbm, smem],
            out_specs=[vmem] * 4,
            scratch_shapes=[
                pltpu.VMEM((NBLK, BLK), f32),
                pltpu.SMEM(decays.shape, f32),
                pltpu.SMEM(widths.shape, f32),
                pltpu.VMEM(mix_start.shape, f32),
                pltpu.SMEM(pair_block.shape, jnp.int32),
                pltpu.SMEM(pair_source.shape, jnp.int32),
                pltpu.VMEM((NBLK, 4, BLK), f32),
                pltpu.VMEM((2, NBLK, 4, BLK), f32),
                pltpu.VMEM((8, BLK), jnp.int32),
                pltpu.VMEM((NEAR, 8, BLK), jnp.int32),
                pltpu.VMEM((2 * BLK, 4 * BLK), jnp.bfloat16),
                pltpu.VMEM((DEPTH - 1, 4 * PMAX, BLK), f32),
                pltpu.VMEM((DEPTH, 4 * PMAX, BLK), f32),
                pltpu.VMEM((PMAX, 4, BLK), f32),
                pltpu.VMEM((PMAX, 4, BLK), f32),
                pltpu.VMEM((PMAX, 3, BLK, BLK), f32),
                pltpu.VMEM((PMAX, NL, 2, BLK, BLK), jnp.bfloat16),
                pltpu.VMEM((PMAX, NK * NL, BLK), f32),
                pltpu.VMEM((PMAX, NK, BLK), f32),
                pltpu.VMEM((PMAX, NK, BLK), f32),
                pltpu.VMEM((2, NL, BLK), f32),
                pltpu.VMEM((2, 4, BLK), f32),
                pltpu.VMEM((2, 2, BLK), f32),
                pltpu.VMEM((2, max(n_tm, n_region), 4, BLK), f32),
                pltpu.VMEM((2, max(n_tm, n_region), 2, BLK), f32),
                pltpu.VMEM((NEAR + 1, 8, BLK), f32),
                dma((7,)),
                dma((NEAR,)),
                dma((NEAR,)),
                dma((2,)),
                dma((2,)),
                dma((DEPTH - 1,)),
                dma((DEPTH - 1,)),
                dma((NEAR,)),
                dma((NEAR,)),
                dma((2 * ITERS,)),
                dma((2 * ITERS,)),
            ],
            compiler_params=pltpu.CompilerParams(
                collective_id=0, has_side_effects=True, vmem_limit_bytes=60 * 2**20
            ),
            name="etas_em",
        )(
            blocks,
            jnp.reshape(background, (NBLK, BLK)),
            decays,
            widths,
            mix_start,
            rate_start,
            pair_block,
            pair_source,
            pair_count,
        )
        mixture, rate, share, offspring = pl.pallas_call(
            finish,
            out_shape=results,
            in_specs=[vmem] * 4,
            out_specs=[hbm] * 4,
            scratch_shapes=[dma((4,))],
            compiler_params=pltpu.CompilerParams(vmem_limit_bytes=2**20),
            name="hand_on",
        )(*found)
        return (
            mixture,
            jnp.reshape(rate, (1,)),
            jnp.reshape(share, (1, 1, NBLK * BLK)),
            jnp.reshape(offspring, (1, 1, NBLK * BLK)),
        )

    placed = (
        P("tm", "region", None, None),
        P("tm", "region", None),
        P(),
        P(),
        P(),
        P(),
        P("tm", "region", None),
        P("tm", "region", None),
        P("tm", "region"),
    )
    return jax.shard_map(
        body,
        mesh=mesh,
        in_specs=placed,
        out_specs=(P(), P(), P("tm", "region", None), P("tm", "region", None)),
        check_vma=False,
    )
```

```python
import math

import jax
import jax.numpy as jnp
from jax import lax
from jax.experimental import pallas as pl
from jax.experimental.pallas import tpu as pltpu
from jax.sharding import PartitionSpec as P

NK = 16
NL = 16
BLK = 128
NBLK = 24
DEPTH = 4
PMAX = 6
ITERS = 2
CELL = 3 * NBLK
NEAR = 3 * DEPTH - 1
PART = 80
RING = 8
FAR = 1.0e6
MESH = pl.DeviceIdType.MESH
PRODUCTIVITY = 1.0


def split_bf16(value):
    high = value.astype(jnp.bfloat16)
    low = (value - high.astype(jnp.float32)).astype(jnp.bfloat16)
    return high, low


def stacked_rows(value):
    high, low = split_bf16(value)
    return jnp.concatenate(
        [
            jnp.concatenate([high, high], axis=1),
            jnp.concatenate([low, jnp.zeros_like(low)], axis=1),
        ],
        axis=0,
    )


def spread_columns(ref, rows):
    for c in range(3):
        tile = jnp.concatenate([row[c : c + 1] for row in rows] + [rows[0][c : c + 1]] * (8 - len(rows)), axis=0)
        turned = jnp.transpose(tile)
        for p in range(len(rows)):
            ref[p, c] = jnp.broadcast_to(turned[:, p : p + 1], (BLK, BLK))


def columns(*rows):
    return jnp.transpose(jnp.concatenate(rows, axis=0))


def kernel(
    n_tm,
    n_region,
    ev_in,
    bg_in,
    decays_in,
    widths_in,
    mix_in,
    rate_s,
    block_in,
    source_in,
    count_s,
    mix_out,
    rate_out,
    share_out,
    offspring_out,
    bg_ref,
    decays_s,
    widths_s,
    mix_ref,
    block_s,
    source_s,
    events,
    beside,
    request,
    requests,
    cells,
    answer,
    picked,
    targets,
    sources,
    target_cols,
    falloff,
    stats,
    early,
    late,
    coeff,
    payload_first,
    payload_last,
    partial_first,
    partial_last,
    returned,
    local_sem,
    request_send,
    request_recv,
    event_send,
    event_recv,
    answer_send,
    answer_recv,
    return_send,
    return_recv,
    sum_send,
    sum_recv,
    ready,
):
    slab = lax.axis_index("tm")
    zone = lax.axis_index("region")
    events_all = float(n_tm * n_region * NBLK * BLK)
    payloads, partials = (payload_first, payload_last), (partial_first, partial_last)

    def wrapped(place, step, length):
        moved = place + step
        return jnp.where(moved >= length, moved - length, jnp.where(moved < 0, moved + length, moved))

    def device(lag, side):
        return (wrapped(slab, lag, n_tm), wrapped(zone, side, n_region))

    x, z = lax.div(slab, RING), lax.div(zone, 2)
    y, core = slab - x * RING, zone - z * 2
    xs, zs = n_tm // RING, n_region // 2

    def hops(*steps):
        return -sum(min(step, length - step) for step, length in steps)

    row = sorted(
        ((dy, dc) for dy in range(RING) for dc in range(2) if dy or dc),
        key=lambda step: hops((step[0], RING)),
    )
    column = sorted(
        ((dx, dz) for dx in range(xs) for dz in range(zs) if dx or dz),
        key=lambda step: hops((step[0], xs), (step[1], zs)),
    )
    peers = (
        [(x * RING + wrapped(y, dy, RING), z * 2 + wrapped(core, dc, 2)) for dy, dc in row],
        [(wrapped(x, dx, xs) * RING + y, wrapped(z, dz, zs) * 2 + core) for dx, dz in column],
    )
    my_place = (y * 2 + core, x * zs + z)

    staged = (
        (source_in, source_s),
        (block_in, block_s),
        (decays_in, decays_s),
        (widths_in, widths_s),
        (mix_in, mix_ref),
        (bg_in, bg_ref),
        (ev_in, events),
    )
    staging = [
        pltpu.make_async_copy(src, dst, local_sem.at[index])
        for index, (src, dst) in enumerate(staged)
    ]
    for copy in staging:
        copy.start()

    barrier = pltpu.get_barrier_semaphore()
    near = [(lag, 0) for lag in range(1, DEPTH)]
    near += [(lag, side) for lag in range(DEPTH) for side in (-1, 1)]
    def inward(place, length):
        return 2 * min(place, length - place) - (1 <= place <= length // 2)

    def inward_of(place, length):
        rank = 0
        for other in range(1, length):
            rank = jnp.where(place == other, inward(other, length), rank)
        return rank

    ranks = (2 * inward_of(y, RING) + 1 - core, xs * z + inward_of(x, xs))
    by_rank = (
        [
            (2 * inward(oy, RING) + 1 - oc, (x * RING + oy, z * 2 + oc))
            for oy in range(RING)
            for oc in range(2)
        ],
        [
            (xs * oz + inward(ox, xs), (ox * RING + y, oz * 2 + core))
            for ox in range(xs)
            for oz in range(zs)
        ],
    )

    def greet(place):
        pl.semaphore_signal(barrier, inc=1, device_id=place, device_id_type=MESH)

    for lag, side in near:
        greet(device(-lag, side))
        if lag:
            greet(device(lag, -side))
    for axis in range(2):
        for rank, place in by_rank[axis]:

            @pl.when(rank > ranks[axis])
            def _():
                greet(place)

    staging[0].wait()
    row8 = lax.broadcasted_iota(jnp.int32, (8, BLK), 0)
    asked = jnp.zeros((8, BLK), jnp.int32)
    for p in range(PMAX):
        asked = jnp.where(row8 == p, source_s[0, 0, p], asked)
    request[...] = asked
    pl.semaphore_wait(barrier, 2 * len(near) - 2 + ranks[0] + ranks[1])

    pending = []

    def send(src, dst, send_sem, recv_sem, device):
        copy = pltpu.make_async_remote_copy(
            src_ref=src,
            dst_ref=dst,
            send_sem=send_sem,
            recv_sem=recv_sem,
            device_id=device,
            device_id_type=MESH,
        )
        copy.start()
        pending.append(copy)
        return copy

    def ask(index):
        lag, side = near[index]
        return send(
            request,
            requests.at[index],
            request_send.at[index],
            request_recv.at[index],
            device(-lag, side),
        )

    askers = DEPTH - 1
    request_copies = [ask(index) for index in range(askers)]

    staging[-1].wait()
    event_copies = [
        send(
            events,
            beside.at[side],
            event_send.at[side],
            event_recv.at[side],
            device(0, 1 - 2 * side),
        )
        for side in range(2)
    ]
    for axis in range(2):
        for rank, place in by_rank[axis]:

            @pl.when(rank < ranks[axis])
            def _():
                pl.semaphore_signal(
                    ready.at[axis], inc=1, device_id=place, device_id_type=MESH
                )

    for copy in staging[1:-1]:
        copy.wait()
    decay_col = jnp.zeros((NK, BLK), jnp.float32)
    row16 = lax.broadcasted_iota(jnp.int32, (NK, BLK), 0)
    for k in range(NK):
        decay_col = jnp.where(row16 == k, decays_s[k], decay_col)
    width_col = jnp.zeros((NL, BLK), jnp.float32)
    for l in range(NL):
        width_col = jnp.where(row16 == l, widths_s[l], width_col)
    spread = 2.0 * width_col * width_col
    coeff[0] = -math.log2(math.e) / spread
    coeff[1] = 1.0 / (math.pi * spread)
    mix_tile = mix_ref[...]
    mixture = [jnp.broadcast_to(mix_tile[:, l : l + 1], (NK, BLK)) for l in range(NL)]
    mixture = jnp.concatenate(mixture, axis=0)
    own_yield = jnp.sum(jnp.exp(PRODUCTIVITY * events[:, 3, :]), axis=0, keepdims=True)
    own_yield = jnp.broadcast_to(jnp.sum(own_yield, axis=1, keepdims=True), (1, BLK))

    start_time = slab.astype(jnp.float32)
    live_count = count_s[0, 0]
    own_targets = [events[block_s[0, 0, p]] for p in range(PMAX)]
    for p, rows in enumerate(own_targets):
        targets[p] = rows
        live = jnp.where(p < live_count, 1.0, 0.0)
        late[p] = decay_col * jnp.exp(-decay_col * (rows[0:1] - start_time)) * live
    spread_columns(target_cols, own_targets)

    lane = lax.broadcasted_iota(jnp.int32, (8, 2 * BLK), 1)

    def one_hot(tile, lag, part):
        named = jnp.concatenate([tile, tile], axis=1) - (lag * CELL - part * PART)
        return jnp.where(named == lane, 1.0, 0.0)

    for copy in event_copies:
        copy.wait_recv()
    for c in range(4):
        value = jnp.concatenate(
            [
                beside[0, :, c, :],
                events[:, c, :],
                beside[1, :, c, :],
                jnp.zeros((PART - CELL, BLK), jnp.float32),
            ],
            axis=0,
        )
        at = slice(c * BLK, (c + 1) * BLK)
        for part in range(3):
            term = value.astype(jnp.bfloat16)
            cells[part * PART : (part + 1) * PART, at] = term
            value = value - term.astype(jnp.float32)
        cells[3 * PART :, at] = jnp.zeros((2 * BLK - 3 * PART, BLK), jnp.bfloat16)
    for copy in request_copies:
        copy.wait_recv()
    tiles = [asked] + [requests[lag - 1] for lag in range(1, DEPTH)]
    wanted = jnp.concatenate(
        [one_hot(tile, lag, part) for part in range(3) for lag, tile in enumerate(tiles)], axis=0
    ).astype(jnp.bfloat16)
    terms = jnp.dot(wanted, cells[...], preferred_element_type=jnp.float32)
    rows = 8 * DEPTH
    found = (terms[:rows] + terms[rows : 2 * rows]) + terms[2 * rows :]
    answer_copies = []
    for lag in range(DEPTH - 1, -1, -1):
        place = picked.at[0] if lag == 0 else answer.at[lag - 1]
        place[...] = jnp.concatenate(
            [found[8 * lag : 8 * lag + PMAX, c * BLK : (c + 1) * BLK] for c in range(4)], axis=0
        )
        if lag:
            answer_copies.append(
                send(
                    place,
                    picked.at[lag],
                    answer_send.at[lag - 1],
                    answer_recv.at[lag - 1],
                    device(lag, 0),
                )
            )
    asked_rows = jnp.concatenate([asked[:PMAX]] * 4, axis=0)
    for copy in answer_copies:
        copy.wait_recv()
    chosen = picked[0]
    for lag in range(1, DEPTH):
        chosen = jnp.where(asked_rows >= lag * CELL, picked[lag], chosen)
    turned = jnp.transpose(chosen)
    for p in range(PMAX):
        rows = [chosen[c * PMAX + p : c * PMAX + p + 1] for c in range(4)]
        sources[p] = jnp.concatenate(rows, axis=0)
        early[p] = jnp.exp(decay_col * (rows[0] - start_time)) * jnp.exp(PRODUCTIVITY * rows[3])

    def distances(target, source):
        gap_time = target[0] - source[0]
        gap_east = target[1] - source[1]
        gap_north = target[2] - source[2]
        square = gap_east * gap_east + gap_north * gap_north
        return jnp.where(gap_time > 0.0, square, FAR)

    def as_rows(value):
        return [value[c : c + 1] for c in range(3)]

    def fall(square, l):
        return split_bf16(jnp.exp2(square * coeff[0, l : l + 1, :]))

    first_rows = []
    for p in range(PMAX):
        after = late[p]
        left = stacked_rows(early[p])
        square = distances(
            as_rows(targets[p]),
            [turned[:, c * PMAX + p : c * PMAX + p + 1] for c in range(3)],
        )
        summed = jnp.zeros((NK, BLK), jnp.float32)
        for pair in range(NL // 2):
            parts = [jnp.concatenate(fall(square, l), axis=0) for l in (2 * pair, 2 * pair + 1)]
            right = jnp.concatenate(parts, axis=1)
            both = jnp.dot(left, right, preferred_element_type=jnp.float32)
            both = both[:NK] + both[NK:]
            for side in range(2):
                l = 2 * pair + side
                tile = both[:, side * BLK : (side + 1) * BLK] * after * coeff[1, l : l + 1, :]
                stats[p, l * NK : (l + 1) * NK, :] = tile
                summed = summed + tile * mixture[l * NK : (l + 1) * NK]
        first_rows.append(jnp.sum(summed, axis=0, keepdims=True))

    def prepare_back(index, carry):
        for p in (2 * index, 2 * index + 1):
            square = distances([target_cols[p, c] for c in range(3)], as_rows(sources[p]))
            for l in range(NL):
                falloff[p, l, 0], falloff[p, l, 1] = fall(square, l)
        return carry

    block_row = lax.broadcasted_iota(jnp.int32, (NBLK, BLK), 0)
    background = bg_ref[...]

    def expect(row_of, rate):
        triggered = jnp.zeros((NBLK, BLK), jnp.float32)
        for p in range(PMAX):
            row = row_of(p)
            triggered = triggered + jnp.where(block_row == block_s[0, 0, p], row, 0.0)
        level = rate * background
        inverse = 1.0 / (level + triggered)
        share = level * inverse
        weights = [
            jnp.sum(jnp.where(block_row == block_s[0, 0, p], inverse, 0.0), axis=0, keepdims=True)
            for p in range(PMAX)
        ]
        scores = stats[0] * weights[0]
        for p in range(1, PMAX):
            scores = scores + stats[p] * weights[p]
        rows = [
            jnp.sum(jnp.transpose(scores[half * BLK : (half + 1) * BLK]), axis=0, keepdims=True)
            for half in range(2)
        ]
        return share, weights, rows

    def start_sum(stage, value):
        sweep, axis = divmod(stage, 2)
        if sweep == 0:
            later = len(peers[axis]) - ranks[axis]

            @pl.when(later > 0)
            def _():
                pl.semaphore_wait(ready.at[axis], later)

        payload, partial = payloads[sweep].at[axis], partials[sweep].at[axis]
        payload[...] = value
        partial[my_place[axis]] = value
        for other in peers[axis]:
            pltpu.make_async_remote_copy(
                src_ref=payload,
                dst_ref=partial.at[my_place[axis]],
                send_sem=sum_send.at[stage],
                recv_sem=sum_recv.at[stage],
                device_id=other,
                device_id_type=MESH,
            ).start()

    def others(stage, sems):
        sweep, axis = divmod(stage, 2)
        part = partials[sweep].at[axis, pl.ds(0, len(peers[axis]))]
        return pltpu.make_async_copy(part, part, sems.at[stage])

    def end_sum(stage):
        sweep, axis = divmod(stage, 2)
        others(stage, sum_recv).wait()
        return jnp.sum(partials[sweep][axis, 0 : len(peers[axis]) + 1], axis=0)

    def update(mixture, total, yield_total):
        cols = columns(*([total] * (8 // total.shape[0])))
        factor = jnp.concatenate(
            [jnp.broadcast_to(cols[:, half : half + 1], (BLK, BLK)) for half in range(2)], axis=0
        )
        mass = mixture * factor
        triggered = jnp.sum(mass, axis=0, keepdims=True)
        return mass * (1.0 / yield_total), 1.0 - triggered / events_all

    share, weights, rows = expect(lambda p: first_rows[p], jnp.full((1, BLK), rate_s[0], jnp.float32))
    value = jnp.concatenate(rows + [own_yield, own_yield], axis=0)
    start_sum(0, value)
    request_copies = [ask(index) for index in range(askers, len(near))]
    lax.fori_loop(0, 2, prepare_back, 0)
    value = end_sum(0)
    start_sum(1, value)
    lax.fori_loop(2, 3, prepare_back, 0)
    for copy in request_copies:
        copy.wait_recv()
    for copy in pending:
        copy.wait_send()
    pending.clear()
    value = end_sum(1)
    yield_total = value[2:3, :]
    mixture, rate = update(mixture, value, yield_total)

    share, weights, rows = expect(
        lambda p: jnp.sum(stats[p] * mixture, axis=0, keepdims=True), rate
    )
    start_sum(2, jnp.concatenate(rows, axis=0))
    share_out[...] = share
    scaled = mixture * jnp.concatenate(
        [jnp.broadcast_to(coeff[1, l : l + 1, :], (NK, BLK)) for l in range(NL)], axis=0
    )

    for p in range(PMAX):
        late[p] = late[p] * weights[p]

    stats[0] = scaled

    def give_back(index, rows):
        for p in (2 * index, 2 * index + 1):
            left = stacked_rows(late[p])
            gathered = jnp.zeros((NK, BLK), jnp.float32)
            for pair in range(NL // 2):
                right = jnp.concatenate(
                    [
                        jnp.concatenate([falloff[p, l, 0], falloff[p, l, 1]], axis=0)
                        for l in (2 * pair, 2 * pair + 1)
                    ],
                    axis=1,
                )
                both = jnp.dot(left, right, preferred_element_type=jnp.float32)
                both = both[:NK] + both[NK:]
                for side in range(2):
                    l = 2 * pair + side
                    gathered = (
                        gathered
                        + both[:, side * BLK : (side + 1) * BLK] * stats[0, l * NK : (l + 1) * NK, :]
                    )
            row = jnp.sum(gathered * early[p], axis=0, keepdims=True)
            rows = jnp.where(lax.broadcasted_iota(jnp.int32, (8, BLK), 0) == p, row, rows)
        return rows

    rows = lax.fori_loop(0, PMAX // 2, give_back, jnp.zeros((8, BLK), jnp.float32))
    returned[0] = rows
    return_copies = [
        send(
            returned.at[0],
            returned.at[index + 1],
            return_send.at[index],
            return_recv.at[index],
            device(-lag, side),
        )
        for index, (lag, side) in enumerate(near)
    ]
    value = end_sum(2)
    start_sum(3, value)

    for copy in return_copies:
        copy.wait_recv()
    gathered = jnp.zeros((NBLK, BLK), jnp.float32)
    for index, (lag, side) in enumerate([(0, 0)] + near):
        first = (lag * 3 + side + 1) * NBLK
        for p in range(PMAX):
            named = asked[p : p + 1] if index == 0 else requests[index - 1, p : p + 1, :]
            gathered = gathered + jnp.where(
                block_row == named - first, returned[index, p : p + 1, :], 0.0
            )
    offspring_out[...] = gathered
    for copy in pending:
        copy.wait_send()
    for stage in range(3):
        others(stage, sum_send).wait()
    value = end_sum(3)
    others(3, sum_send).wait()
    mixture, rate = update(mixture, value, yield_total)
    lane16 = lax.broadcasted_iota(jnp.int32, (NK, BLK), 1)
    square_mix = jnp.zeros((NK, BLK), jnp.float32)
    for l in range(NL):
        square_mix = jnp.where(lane16 == l, mixture[l * NK : (l + 1) * NK], square_mix)
    mix_out[...] = square_mix[:, :NL]
    rate_out[...] = rate[:, 0:1]


def finish(*refs):
    arrived, handed, sems = refs[:4], refs[4:8], refs[8]
    copies = [
        pltpu.make_async_copy(src, dst, sems.at[index])
        for index, (src, dst) in enumerate(zip(arrived, handed))
    ]
    for copy in copies:
        copy.start()
    for copy in copies:
        copy.wait()


def solution(mesh):
    n_tm, n_region = mesh.shape["tm"], mesh.shape["region"]

    def body(
        events, background, decays, widths, mix_start, rate_start, pair_block, pair_source, pair_count
    ):
        blocks = jnp.transpose(jnp.reshape(events, (4, NBLK, BLK)), (1, 0, 2))
        smem = pl.BlockSpec(memory_space=pltpu.SMEM)
        hbm = pl.BlockSpec(memory_space=pltpu.HBM)
        vmem = pl.BlockSpec(memory_space=pltpu.VMEM)
        f32 = jnp.float32
        dma = pltpu.SemaphoreType.DMA
        results = [
            jax.ShapeDtypeStruct((NK, NL), f32),
            jax.ShapeDtypeStruct((1, 1), f32),
            jax.ShapeDtypeStruct((NBLK, BLK), f32),
            jax.ShapeDtypeStruct((NBLK, BLK), f32),
        ]
        found = pl.pallas_call(
            lambda *refs: kernel(n_tm, n_region, *refs),
            out_shape=[pltpu.VMEM(leaf.shape, leaf.dtype) for leaf in results],
            in_specs=[hbm] * 5 + [smem, hbm, hbm, smem],
            out_specs=[vmem] * 4,
            scratch_shapes=[
                pltpu.VMEM((NBLK, BLK), f32),
                pltpu.SMEM(decays.shape, f32),
                pltpu.SMEM(widths.shape, f32),
                pltpu.VMEM(mix_start.shape, f32),
                pltpu.SMEM(pair_block.shape, jnp.int32),
                pltpu.SMEM(pair_source.shape, jnp.int32),
                pltpu.VMEM((NBLK, 4, BLK), f32),
                pltpu.VMEM((2, NBLK, 4, BLK), f32),
                pltpu.VMEM((8, BLK), jnp.int32),
                pltpu.VMEM((NEAR, 8, BLK), jnp.int32),
                pltpu.VMEM((2 * BLK, 4 * BLK), jnp.bfloat16),
                pltpu.VMEM((DEPTH - 1, 4 * PMAX, BLK), f32),
                pltpu.VMEM((DEPTH, 4 * PMAX, BLK), f32),
                pltpu.VMEM((PMAX, 4, BLK), f32),
                pltpu.VMEM((PMAX, 4, BLK), f32),
                pltpu.VMEM((PMAX, 3, BLK, BLK), f32),
                pltpu.VMEM((PMAX, NL, 2, BLK, BLK), jnp.bfloat16),
                pltpu.VMEM((PMAX, NK * NL, BLK), f32),
                pltpu.VMEM((PMAX, NK, BLK), f32),
                pltpu.VMEM((PMAX, NK, BLK), f32),
                pltpu.VMEM((2, NL, BLK), f32),
                pltpu.VMEM((2, 4, BLK), f32),
                pltpu.VMEM((2, 2, BLK), f32),
                pltpu.VMEM((2, max(n_tm, n_region), 4, BLK), f32),
                pltpu.VMEM((2, max(n_tm, n_region), 2, BLK), f32),
                pltpu.VMEM((NEAR + 1, 8, BLK), f32),
                dma((7,)),
                dma((NEAR,)),
                dma((NEAR,)),
                dma((2,)),
                dma((2,)),
                dma((DEPTH - 1,)),
                dma((DEPTH - 1,)),
                dma((NEAR,)),
                dma((NEAR,)),
                dma((2 * ITERS,)),
                dma((2 * ITERS,)),
                pltpu.SemaphoreType.REGULAR((2,)),
            ],
            compiler_params=pltpu.CompilerParams(
                collective_id=0, has_side_effects=True, vmem_limit_bytes=60 * 2**20
            ),
            name="etas_em",
        )(
            blocks,
            jnp.reshape(background, (NBLK, BLK)),
            decays,
            widths,
            mix_start,
            rate_start,
            pair_block,
            pair_source,
            pair_count,
        )
        mixture, rate, share, offspring = pl.pallas_call(
            finish,
            out_shape=results,
            in_specs=[vmem] * 4,
            out_specs=[hbm] * 4,
            scratch_shapes=[dma((4,))],
            compiler_params=pltpu.CompilerParams(vmem_limit_bytes=2**20),
            name="hand_on",
        )(*found)
        return (
            mixture,
            jnp.reshape(rate, (1,)),
            jnp.reshape(share, (1, 1, NBLK * BLK)),
            jnp.reshape(offspring, (1, 1, NBLK * BLK)),
        )

    placed = (
        P("tm", "region", None, None),
        P("tm", "region", None),
        P(),
        P(),
        P(),
        P(),
        P("tm", "region", None),
        P("tm", "region", None),
        P("tm", "region"),
    )
    return jax.shard_map(
        body,
        mesh=mesh,
        in_specs=placed,
        out_specs=(P(), P(), P("tm", "region", None), P("tm", "region", None)),
        check_vma=False,
    )
```

```python
import math

import jax
import jax.numpy as jnp
from jax import lax
from jax.experimental import pallas as pl
from jax.experimental.pallas import tpu as pltpu
from jax.sharding import PartitionSpec as P

NK = 16
NL = 16
BLK = 128
NBLK = 24
DEPTH = 4
PMAX = 6
ITERS = 2
CELL = 3 * NBLK
NEAR = 3 * DEPTH - 1
PART = 80
RING = 8
FAR = 1.0e6
MESH = pl.DeviceIdType.MESH
PRODUCTIVITY = 1.0


def split_bf16(value):
    high = value.astype(jnp.bfloat16)
    low = (value - high.astype(jnp.float32)).astype(jnp.bfloat16)
    return high, low


def stacked_rows(value):
    high, low = split_bf16(value)
    return jnp.concatenate(
        [
            jnp.concatenate([high, high], axis=1),
            jnp.concatenate([low, jnp.zeros_like(low)], axis=1),
        ],
        axis=0,
    )


def spread_columns(ref, rows):
    for c in range(3):
        tile = jnp.concatenate([row[c : c + 1] for row in rows] + [rows[0][c : c + 1]] * (8 - len(rows)), axis=0)
        turned = jnp.transpose(tile)
        for p in range(len(rows)):
            ref[p, c] = jnp.broadcast_to(turned[:, p : p + 1], (BLK, BLK))


def columns(*rows):
    return jnp.transpose(jnp.concatenate(rows, axis=0))


def kernel(
    n_tm,
    n_region,
    ev_in,
    bg_in,
    decays_in,
    widths_in,
    mix_in,
    rate_s,
    block_in,
    source_in,
    count_s,
    mix_out,
    rate_out,
    share_out,
    offspring_out,
    bg_ref,
    decays_s,
    widths_s,
    mix_ref,
    block_s,
    source_s,
    events,
    beside,
    request,
    requests,
    cells,
    answer,
    picked,
    targets,
    sources,
    target_cols,
    falloff,
    stats,
    early,
    late,
    coeff,
    payload_first,
    payload_last,
    partial_first,
    partial_last,
    returned,
    local_sem,
    request_send,
    request_recv,
    event_send,
    event_recv,
    answer_send,
    answer_recv,
    return_send,
    return_recv,
    sum_send,
    sum_recv,
):
    slab = lax.axis_index("tm")
    zone = lax.axis_index("region")
    events_all = float(n_tm * n_region * NBLK * BLK)
    payloads, partials = (payload_first, payload_last), (partial_first, partial_last)

    def wrapped(place, step, length):
        moved = place + step
        return jnp.where(moved >= length, moved - length, jnp.where(moved < 0, moved + length, moved))

    def device(lag, side):
        return (wrapped(slab, lag, n_tm), wrapped(zone, side, n_region))

    x, z = lax.div(slab, RING), lax.div(zone, 2)
    y, core = slab - x * RING, zone - z * 2
    xs, zs = n_tm // RING, n_region // 2

    def hops(*steps):
        return -sum(min(step, length - step) for step, length in steps)

    row = sorted(
        ((dy, dc) for dy in range(RING) for dc in range(2) if dy or dc),
        key=lambda step: hops((step[0], RING)),
    )
    column = sorted(
        ((dx, dz) for dx in range(xs) for dz in range(zs) if dx or dz),
        key=lambda step: hops((step[0], xs), (step[1], zs)),
    )
    peers = (
        [(x * RING + wrapped(y, dy, RING), z * 2 + wrapped(core, dc, 2)) for dy, dc in row],
        [(wrapped(x, dx, xs) * RING + y, wrapped(z, dz, zs) * 2 + core) for dx, dz in column],
    )
    my_place = (y * 2 + core, x * zs + z)

    staged = (
        (source_in, source_s),
        (block_in, block_s),
        (decays_in, decays_s),
        (widths_in, widths_s),
        (mix_in, mix_ref),
        (bg_in, bg_ref),
        (ev_in, events),
    )
    staging = [
        pltpu.make_async_copy(src, dst, local_sem.at[index])
        for index, (src, dst) in enumerate(staged)
    ]
    for copy in staging:
        copy.start()

    barrier = pltpu.get_barrier_semaphore()
    near = [(lag, 0) for lag in range(1, DEPTH)]
    near += [(lag, side) for lag in range(DEPTH) for side in (-1, 1)]
    greeted = [
        (hops((step[0], RING)), place) for step, place in zip(row, peers[0])
    ] + [
        (hops((step[0], xs), (step[1], zs)), place) for step, place in zip(column, peers[1])
    ]
    for lag, side in near:
        greeted.append((-lag - abs(side), device(-lag, side)))
        if lag:
            greeted.append((-lag - abs(side), device(lag, -side)))
    for _, place in sorted(greeted, key=lambda entry: entry[0]):
        pl.semaphore_signal(barrier, inc=1, device_id=place, device_id_type=MESH)
    staging[0].wait()
    row8 = lax.broadcasted_iota(jnp.int32, (8, BLK), 0)
    asked = jnp.zeros((8, BLK), jnp.int32)
    for p in range(PMAX):
        asked = jnp.where(row8 == p, source_s[0, 0, p], asked)
    request[...] = asked
    pl.semaphore_wait(barrier, len(greeted))

    pending = []

    def send(src, dst, send_sem, recv_sem, device):
        copy = pltpu.make_async_remote_copy(
            src_ref=src,
            dst_ref=dst,
            send_sem=send_sem,
            recv_sem=recv_sem,
            device_id=device,
            device_id_type=MESH,
        )
        copy.start()
        pending.append(copy)
        return copy

    def ask(index):
        lag, side = near[index]
        return send(
            request,
            requests.at[index],
            request_send.at[index],
            request_recv.at[index],
            device(-lag, side),
        )

    askers = DEPTH - 1
    request_copies = [ask(index) for index in range(askers)]

    staging[-1].wait()
    event_copies = [
        send(
            events,
            beside.at[side],
            event_send.at[side],
            event_recv.at[side],
            device(0, 1 - 2 * side),
        )
        for side in range(2)
    ]
    for copy in staging[1:-1]:
        copy.wait()
    decay_col = jnp.zeros((NK, BLK), jnp.float32)
    row16 = lax.broadcasted_iota(jnp.int32, (NK, BLK), 0)
    for k in range(NK):
        decay_col = jnp.where(row16 == k, decays_s[k], decay_col)
    width_col = jnp.zeros((NL, BLK), jnp.float32)
    for l in range(NL):
        width_col = jnp.where(row16 == l, widths_s[l], width_col)
    spread = 2.0 * width_col * width_col
    coeff[0] = -math.log2(math.e) / spread
    coeff[1] = 1.0 / (math.pi * spread)
    mix_tile = mix_ref[...]
    mixture = [jnp.broadcast_to(mix_tile[:, l : l + 1], (NK, BLK)) for l in range(NL)]
    mixture = jnp.concatenate(mixture, axis=0)
    own_yield = jnp.sum(jnp.exp(PRODUCTIVITY * events[:, 3, :]), axis=0, keepdims=True)
    own_yield = jnp.broadcast_to(jnp.sum(own_yield, axis=1, keepdims=True), (1, BLK))

    start_time = slab.astype(jnp.float32)
    live_count = count_s[0, 0]
    own_targets = [events[block_s[0, 0, p]] for p in range(PMAX)]
    for p, rows in enumerate(own_targets):
        targets[p] = rows
        live = jnp.where(p < live_count, 1.0, 0.0)
        late[p] = decay_col * jnp.exp(-decay_col * (rows[0:1] - start_time)) * live
    spread_columns(target_cols, own_targets)

    lane = lax.broadcasted_iota(jnp.int32, (8, 2 * BLK), 1)

    def one_hot(tile, lag, part):
        named = jnp.concatenate([tile, tile], axis=1) - (lag * CELL - part * PART)
        return jnp.where(named == lane, 1.0, 0.0)

    for copy in event_copies:
        copy.wait_recv()
    for c in range(4):
        value = jnp.concatenate(
            [
                beside[0, :, c, :],
                events[:, c, :],
                beside[1, :, c, :],
                jnp.zeros((PART - CELL, BLK), jnp.float32),
            ],
            axis=0,
        )
        at = slice(c * BLK, (c + 1) * BLK)
        for part in range(3):
            term = value.astype(jnp.bfloat16)
            cells[part * PART : (part + 1) * PART, at] = term
            value = value - term.astype(jnp.float32)
        cells[3 * PART :, at] = jnp.zeros((2 * BLK - 3 * PART, BLK), jnp.bfloat16)
    for copy in request_copies:
        copy.wait_recv()
    tiles = [asked] + [requests[lag - 1] for lag in range(1, DEPTH)]
    wanted = jnp.concatenate(
        [one_hot(tile, lag, part) for part in range(3) for lag, tile in enumerate(tiles)], axis=0
    ).astype(jnp.bfloat16)
    terms = jnp.dot(wanted, cells[...], preferred_element_type=jnp.float32)
    rows = 8 * DEPTH
    found = (terms[:rows] + terms[rows : 2 * rows]) + terms[2 * rows :]
    answer_copies = []
    for lag in range(DEPTH - 1, -1, -1):
        place = picked.at[0] if lag == 0 else answer.at[lag - 1]
        place[...] = jnp.concatenate(
            [found[8 * lag : 8 * lag + PMAX, c * BLK : (c + 1) * BLK] for c in range(4)], axis=0
        )
        if lag:
            answer_copies.append(
                send(
                    place,
                    picked.at[lag],
                    answer_send.at[lag - 1],
                    answer_recv.at[lag - 1],
                    device(lag, 0),
                )
            )
    asked_rows = jnp.concatenate([asked[:PMAX]] * 4, axis=0)
    for copy in answer_copies:
        copy.wait_recv()
    chosen = picked[0]
    for lag in range(1, DEPTH):
        chosen = jnp.where(asked_rows >= lag * CELL, picked[lag], chosen)
    turned = jnp.transpose(chosen)
    for p in range(PMAX):
        rows = [chosen[c * PMAX + p : c * PMAX + p + 1] for c in range(4)]
        sources[p] = jnp.concatenate(rows, axis=0)
        early[p] = jnp.exp(decay_col * (rows[0] - start_time)) * jnp.exp(PRODUCTIVITY * rows[3])

    def distances(target, source):
        gap_time = target[0] - source[0]
        gap_east = target[1] - source[1]
        gap_north = target[2] - source[2]
        square = gap_east * gap_east + gap_north * gap_north
        return jnp.where(gap_time > 0.0, square, FAR)

    def as_rows(value):
        return [value[c : c + 1] for c in range(3)]

    def fall(square, l):
        return split_bf16(jnp.exp2(square * coeff[0, l : l + 1, :]))

    first_rows = []
    for p in range(PMAX):
        after = late[p]
        left = stacked_rows(early[p])
        square = distances(
            as_rows(targets[p]),
            [turned[:, c * PMAX + p : c * PMAX + p + 1] for c in range(3)],
        )
        summed = jnp.zeros((NK, BLK), jnp.float32)
        for pair in range(NL // 2):
            parts = [jnp.concatenate(fall(square, l), axis=0) for l in (2 * pair, 2 * pair + 1)]
            right = jnp.concatenate(parts, axis=1)
            both = jnp.dot(left, right, preferred_element_type=jnp.float32)
            both = both[:NK] + both[NK:]
            for side in range(2):
                l = 2 * pair + side
                tile = both[:, side * BLK : (side + 1) * BLK] * after * coeff[1, l : l + 1, :]
                stats[p, l * NK : (l + 1) * NK, :] = tile
                summed = summed + tile * mixture[l * NK : (l + 1) * NK]
        first_rows.append(jnp.sum(summed, axis=0, keepdims=True))

    def prepare_back(index, carry):
        for p in (2 * index, 2 * index + 1):
            square = distances([target_cols[p, c] for c in range(3)], as_rows(sources[p]))
            for l in range(NL):
                falloff[p, l, 0], falloff[p, l, 1] = fall(square, l)
        return carry

    block_row = lax.broadcasted_iota(jnp.int32, (NBLK, BLK), 0)
    background = bg_ref[...]

    def expect(row_of, rate):
        triggered = jnp.zeros((NBLK, BLK), jnp.float32)
        for p in range(PMAX):
            row = row_of(p)
            triggered = triggered + jnp.where(block_row == block_s[0, 0, p], row, 0.0)
        level = rate * background
        inverse = 1.0 / (level + triggered)
        share = level * inverse
        weights = [
            jnp.sum(jnp.where(block_row == block_s[0, 0, p], inverse, 0.0), axis=0, keepdims=True)
            for p in range(PMAX)
        ]
        scores = stats[0] * weights[0]
        for p in range(1, PMAX):
            scores = scores + stats[p] * weights[p]
        rows = [
            jnp.sum(jnp.transpose(scores[half * BLK : (half + 1) * BLK]), axis=0, keepdims=True)
            for half in range(2)
        ]
        return share, weights, rows

    def start_sum(stage, value):
        sweep, axis = divmod(stage, 2)
        payload, partial = payloads[sweep].at[axis], partials[sweep].at[axis]
        payload[...] = value
        for other in peers[axis]:
            pltpu.make_async_remote_copy(
                src_ref=payload,
                dst_ref=partial.at[my_place[axis]],
                send_sem=sum_send.at[stage],
                recv_sem=sum_recv.at[stage],
                device_id=other,
                device_id_type=MESH,
            ).start()
        partial[my_place[axis]] = value

    def others(stage, sems):
        sweep, axis = divmod(stage, 2)
        part = partials[sweep].at[axis, pl.ds(0, len(peers[axis]))]
        return pltpu.make_async_copy(part, part, sems.at[stage])

    def end_sum(stage):
        sweep, axis = divmod(stage, 2)
        others(stage, sum_recv).wait()
        return jnp.sum(partials[sweep][axis, 0 : len(peers[axis]) + 1], axis=0)

    def update(mixture, total, yield_total):
        cols = columns(*([total] * (8 // total.shape[0])))
        factor = jnp.concatenate(
            [jnp.broadcast_to(cols[:, half : half + 1], (BLK, BLK)) for half in range(2)], axis=0
        )
        mass = mixture * factor
        triggered = jnp.sum(mass, axis=0, keepdims=True)
        return mass * (1.0 / yield_total), 1.0 - triggered / events_all

    share, weights, rows = expect(lambda p: first_rows[p], jnp.full((1, BLK), rate_s[0], jnp.float32))
    value = jnp.concatenate(rows + [own_yield, own_yield], axis=0)
    start_sum(0, value)
    request_copies = [ask(index) for index in range(askers, len(near))]
    lax.fori_loop(0, 2, prepare_back, 0)
    value = end_sum(0)
    start_sum(1, value)
    lax.fori_loop(2, 3, prepare_back, 0)
    for copy in request_copies:
        copy.wait_recv()
    for copy in pending:
        copy.wait_send()
    pending.clear()
    value = end_sum(1)
    yield_total = value[2:3, :]
    mixture, rate = update(mixture, value, yield_total)

    share, weights, rows = expect(
        lambda p: jnp.sum(stats[p] * mixture, axis=0, keepdims=True), rate
    )
    start_sum(2, jnp.concatenate(rows, axis=0))
    share_out[...] = share
    scaled = mixture * jnp.concatenate(
        [jnp.broadcast_to(coeff[1, l : l + 1, :], (NK, BLK)) for l in range(NL)], axis=0
    )

    for p in range(PMAX):
        late[p] = late[p] * weights[p]

    stats[0] = scaled

    def give_back(index, rows):
        for p in (2 * index, 2 * index + 1):
            left = stacked_rows(late[p])
            gathered = jnp.zeros((NK, BLK), jnp.float32)
            for pair in range(NL // 2):
                right = jnp.concatenate(
                    [
                        jnp.concatenate([falloff[p, l, 0], falloff[p, l, 1]], axis=0)
                        for l in (2 * pair, 2 * pair + 1)
                    ],
                    axis=1,
                )
                both = jnp.dot(left, right, preferred_element_type=jnp.float32)
                both = both[:NK] + both[NK:]
                for side in range(2):
                    l = 2 * pair + side
                    gathered = (
                        gathered
                        + both[:, side * BLK : (side + 1) * BLK] * stats[0, l * NK : (l + 1) * NK, :]
                    )
            row = jnp.sum(gathered * early[p], axis=0, keepdims=True)
            rows = jnp.where(lax.broadcasted_iota(jnp.int32, (8, BLK), 0) == p, row, rows)
        return rows

    rows = lax.fori_loop(0, PMAX // 2, give_back, jnp.zeros((8, BLK), jnp.float32))
    returned[0] = rows
    return_copies = [
        send(
            returned.at[0],
            returned.at[index + 1],
            return_send.at[index],
            return_recv.at[index],
            device(-lag, side),
        )
        for index, (lag, side) in enumerate(near)
    ]
    value = end_sum(2)
    start_sum(3, value)

    for copy in return_copies:
        copy.wait_recv()
    gathered = jnp.zeros((NBLK, BLK), jnp.float32)
    for index, (lag, side) in enumerate([(0, 0)] + near):
        first = (lag * 3 + side + 1) * NBLK
        for p in range(PMAX):
            named = asked[p : p + 1] if index == 0 else requests[index - 1, p : p + 1, :]
            gathered = gathered + jnp.where(
                block_row == named - first, returned[index, p : p + 1, :], 0.0
            )
    offspring_out[...] = gathered
    for copy in pending:
        copy.wait_send()
    for stage in range(3):
        others(stage, sum_send).wait()
    value = end_sum(3)
    others(3, sum_send).wait()
    mixture, rate = update(mixture, value, yield_total)
    lane16 = lax.broadcasted_iota(jnp.int32, (NK, BLK), 1)
    square_mix = jnp.zeros((NK, BLK), jnp.float32)
    for l in range(NL):
        square_mix = jnp.where(lane16 == l, mixture[l * NK : (l + 1) * NK], square_mix)
    mix_out[...] = square_mix[:, :NL]
    rate_out[...] = rate[:, 0:1]


def finish(*refs):
    arrived, handed, sems = refs[:4], refs[4:8], refs[8]
    copies = [
        pltpu.make_async_copy(src, dst, sems.at[index])
        for index, (src, dst) in enumerate(zip(arrived, handed))
    ]
    for copy in copies:
        copy.start()
    for copy in copies:
        copy.wait()


def solution(mesh):
    n_tm, n_region = mesh.shape["tm"], mesh.shape["region"]

    def body(
        events, background, decays, widths, mix_start, rate_start, pair_block, pair_source, pair_count
    ):
        blocks = jnp.transpose(jnp.reshape(events, (4, NBLK, BLK)), (1, 0, 2))
        smem = pl.BlockSpec(memory_space=pltpu.SMEM)
        hbm = pl.BlockSpec(memory_space=pltpu.HBM)
        vmem = pl.BlockSpec(memory_space=pltpu.VMEM)
        f32 = jnp.float32
        dma = pltpu.SemaphoreType.DMA
        results = [
            jax.ShapeDtypeStruct((NK, NL), f32),
            jax.ShapeDtypeStruct((1, 1), f32),
            jax.ShapeDtypeStruct((NBLK, BLK), f32),
            jax.ShapeDtypeStruct((NBLK, BLK), f32),
        ]
        found = pl.pallas_call(
            lambda *refs: kernel(n_tm, n_region, *refs),
            out_shape=[pltpu.VMEM(leaf.shape, leaf.dtype) for leaf in results],
            in_specs=[hbm] * 5 + [smem, hbm, hbm, smem],
            out_specs=[vmem] * 4,
            scratch_shapes=[
                pltpu.VMEM((NBLK, BLK), f32),
                pltpu.SMEM(decays.shape, f32),
                pltpu.SMEM(widths.shape, f32),
                pltpu.VMEM(mix_start.shape, f32),
                pltpu.SMEM(pair_block.shape, jnp.int32),
                pltpu.SMEM(pair_source.shape, jnp.int32),
                pltpu.VMEM((NBLK, 4, BLK), f32),
                pltpu.VMEM((2, NBLK, 4, BLK), f32),
                pltpu.VMEM((8, BLK), jnp.int32),
                pltpu.VMEM((NEAR, 8, BLK), jnp.int32),
                pltpu.VMEM((2 * BLK, 4 * BLK), jnp.bfloat16),
                pltpu.VMEM((DEPTH - 1, 4 * PMAX, BLK), f32),
                pltpu.VMEM((DEPTH, 4 * PMAX, BLK), f32),
                pltpu.VMEM((PMAX, 4, BLK), f32),
                pltpu.VMEM((PMAX, 4, BLK), f32),
                pltpu.VMEM((PMAX, 3, BLK, BLK), f32),
                pltpu.VMEM((PMAX, NL, 2, BLK, BLK), jnp.bfloat16),
                pltpu.VMEM((PMAX, NK * NL, BLK), f32),
                pltpu.VMEM((PMAX, NK, BLK), f32),
                pltpu.VMEM((PMAX, NK, BLK), f32),
                pltpu.VMEM((2, NL, BLK), f32),
                pltpu.VMEM((2, 4, BLK), f32),
                pltpu.VMEM((2, 2, BLK), f32),
                pltpu.VMEM((2, max(n_tm, n_region), 4, BLK), f32),
                pltpu.VMEM((2, max(n_tm, n_region), 2, BLK), f32),
                pltpu.VMEM((NEAR + 1, 8, BLK), f32),
                dma((7,)),
                dma((NEAR,)),
                dma((NEAR,)),
                dma((2,)),
                dma((2,)),
                dma((DEPTH - 1,)),
                dma((DEPTH - 1,)),
                dma((NEAR,)),
                dma((NEAR,)),
                dma((2 * ITERS,)),
                dma((2 * ITERS,)),
            ],
            compiler_params=pltpu.CompilerParams(
                collective_id=0, has_side_effects=True, vmem_limit_bytes=60 * 2**20
            ),
            name="etas_em",
        )(
            blocks,
            jnp.reshape(background, (NBLK, BLK)),
            decays,
            widths,
            mix_start,
            rate_start,
            pair_block,
            pair_source,
            pair_count,
        )
        mixture, rate, share, offspring = pl.pallas_call(
            finish,
            out_shape=results,
            in_specs=[vmem] * 4,
            out_specs=[hbm] * 4,
            scratch_shapes=[dma((4,))],
            compiler_params=pltpu.CompilerParams(vmem_limit_bytes=2**20),
            name="hand_on",
        )(*found)
        return (
            mixture,
            jnp.reshape(rate, (1,)),
            jnp.reshape(share, (1, 1, NBLK * BLK)),
            jnp.reshape(offspring, (1, 1, NBLK * BLK)),
        )

    placed = (
        P("tm", "region", None, None),
        P("tm", "region", None),
        P(),
        P(),
        P(),
        P(),
        P("tm", "region", None),
        P("tm", "region", None),
        P("tm", "region"),
    )
    return jax.shard_map(
        body,
        mesh=mesh,
        in_specs=placed,
        out_specs=(P(), P(), P("tm", "region", None), P("tm", "region", None)),
        check_vma=False,
    )
```
